32 devices in a mesh: dp: 2 (over x), expert: 16 (over z, y, core).
Axes of the slice: x: 2, y: 2, z: 4, core: 2. Of those that a mesh axis runs over, the one named last changes fastest.
Arguments:
- tokens: bfloat16 [64, 4096], P('expert', 'dp'), may hold values from -6 to 6
- dest_device: int32 [64, 8], P('expert'), may hold values from 0 to 15, all different within a row; in each aligned block of 4 rows (0 to 3, 4 to 7, ...) at most 4 rows name the same one
- local_slot: int32 [64, 8], P('expert'), may hold values from 0 to 2
- route_weights: float32 [64, 8], P('expert'), may hold values from 0.05 to 1
- copy_pick: int32 [16, 1], P('expert'), may hold values from 0 to 1
- w_in: bfloat16 [32, 4096, 2, 1024], P('expert', 'dp'), may hold values from -0.09375 to 0.09375
- w_out: bfloat16 [32, 1024, 4096], P('expert', None, 'dp'), may hold values from -0.1875 to 0.1875
- shared_in: bfloat16 [4096, 2, 2048], P('dp'), may hold values from -0.09375 to 0.09375
- shared_out: bfloat16 [2048, 4096], P(None, 'dp'), may hold values from -0.125 to 0.125
Outputs:
- layer_out: bfloat16 [64, 4096], P('expert', 'dp')
The draws below stay inside these ranges and needn't reach their ends.
Inputs may be any that keep to these rules, and one draw needn't show every extreme that they name: `dest_device`: each row names 8 different indices; among the 4 rows of one device no index is named by more than 4 rows, a bound that some block reaches.
All inputs are finite; a program needn't handle non-finite values.
Results may differ from the reference program's by a relative error of at most 0.02.
Values may be sent and summed in bfloat16 or wider, within the bound.
A program may use at most 128 MiB of HBM per device.

```python
import math
import jax
import jax.numpy as jnp
import numpy as np
from jax import lax

D = 4096
FF = 1024
SFF = 2048
EXP_DEV = 2
REP_DEV = 1
TOP = 8
ROWS_DEV = 4
SLOTS = 3
EXPERTS = 32
SEND = 4
ROWS = 64
N_DP = 2
N_EXPERT = 16


def touch_ends(entries, key, least, top_value):
    shape = entries.shape
    index_at = [jax.random.randint(jax.random.fold_in(key, axis), (), 0, shape[axis]) for axis in range(len(shape))]
    entries = entries.at[tuple(index_at)].set(least)
    longest = shape.index(max(shape))
    index_at[longest] = (index_at[longest] + 1) % shape[longest]
    return entries.at[tuple(index_at)].set(top_value)


def block_levels(rng, extent, shards, low, high):
    factor_of, own = 1.0, jax.random.fold_in(rng, 6)
    for dim, blocks in shards:
        heights = jnp.exp(jax.random.uniform(jax.random.fold_in(own, dim), (blocks,), jnp.float32, low / len(shards), high / len(shards)))
        factor_of = factor_of * jnp.repeat(heights, extent[dim] // blocks).reshape([-1 if axis == dim else 1 for axis in range(len(extent))])
    return factor_of


def deal_out(key, own, number, rows, number_of, top, reach, slope):
    order = jax.random.permutation(key, number_of)
    packed, usual = load_shares(number_of, rows * top, reach, slope, True), load_shares(number_of, rows * top, reach, slope, False)
    places = jnp.arange(number_of)

    def named(lengths, offset_by):
        used = int((lengths > 0).sum())
        fixed = max(1, used // 4)
        moved = fixed + (places - fixed + offset_by * (used - fixed)) % max(1, number_of - fixed)
        return jnp.zeros((number_of,), jnp.int32).at[order[jnp.where(places < fixed, places, moved)]].set(jnp.asarray(lengths, jnp.int32))

    lengths = jnp.where(number % 4 == 0, named(packed, number // 4), named(usual, number - number // 4 - 1))
    mixed = jax.random.permutation(jax.random.fold_in(own, 3), number_of)
    donor, taker = mixed[0:number_of // 2 * 2:2], mixed[1:number_of // 2 * 2:2]
    room = jnp.minimum(lengths[donor] - 1, reach - lengths[taker]) // 2
    room = jnp.where((donor == order[0]) | (taker == order[0]) | (lengths[taker] == 0), 0, jnp.maximum(room, 0))
    moved = jax.random.randint(jax.random.fold_in(own, 4), (number_of // 2,), 0, 1 << 20) % (room + 1)
    lengths = lengths.at[donor].add(-moved).at[taker].add(moved)
    members = jnp.searchsorted(jnp.cumsum(lengths), jnp.arange(rows * top), side="right").astype(jnp.int32)
    table = members.reshape(top, rows).T
    table = table[jax.random.permutation(jax.random.fold_in(own, 1), rows)]
    offset_by = jax.random.randint(jax.random.fold_in(own, 2), (rows, 1), 0, top)
    return jnp.take_along_axis(table, (jnp.arange(top)[None, :] + offset_by) % top, axis=1)


def load_shares(count, total, bound, slope, full):
    portions = [(1 << 20) // math.isqrt(rank ** slope) + 1 for rank in range(1, count + 1)]
    largest = bound if full else min(bound, max(-(-total // count), total * portions[0] // sum(portions)))
    least = 1 if total - largest >= count - 1 else 0
    given, spare = [largest] + [least] * (count - 1), total - largest - least * (count - 1)
    while spare > 0:
        candidates = [i for i in range(1, count) if given[i] < largest] or [i for i in range(1, count) if given[i] < bound]
        pool, remaining = sum([portions[i] for i in candidates]), spare
        for i in candidates:
            more = min(bound - given[i], max(1, remaining * portions[i] // pool), spare)
            given[i] = given[i] + more
            spare = spare - more
    return np.array(given)


def noise(key, dims, scale, limit, cuts=(), held_as=jnp.bfloat16):
    values = scale * jax.random.normal(key, dims, jnp.float32)
    if cuts:
        values = values * block_levels(key, dims, cuts, -0.22, 0.18)
    return jnp.clip(values, -limit, limit).astype(held_as)


def setup_inputs(seed: int = 0) -> dict:
    seeds = jax.random.split(jax.random.key(seed), 10)
    tokens = noise(seeds[0], (ROWS, D), 1.0, 6.0, ((0, 16), (1, 2)))
    dest_device_keys = jax.random.split(jax.random.fold_in(seeds[1], 1), ROWS // ROWS_DEV)
    dest_device_turns = jax.random.permutation(jax.random.fold_in(seeds[1], 3), ROWS // ROWS_DEV)
    dest_device = jax.vmap(lambda own, number: deal_out(jax.random.fold_in(seeds[1], 2), own, number, ROWS_DEV, N_EXPERT, TOP, SEND, 2))(dest_device_keys, dest_device_turns).reshape((ROWS, TOP))
    local_slot = touch_ends(jax.random.randint(seeds[2], (ROWS, TOP), 0, SLOTS), jax.random.fold_in(seeds[2], 1), 0, SLOTS - 1).astype(jnp.int32)
    route_weights = jnp.clip(jnp.exp(math.log(1.0) - 2.9957323 * jax.random.uniform(seeds[3], (ROWS, TOP), jnp.float32) ** block_levels(seeds[3], (ROWS, TOP), ((0, 16),), -0.2, 0.2)), 0.05, 1.0)
    copy_pick = touch_ends(jax.random.randint(seeds[4], (N_EXPERT, REP_DEV), 0, EXP_DEV), jax.random.fold_in(seeds[4], 1), 0, EXP_DEV - 1).astype(jnp.int32)
    w_in = noise(seeds[5], (EXPERTS, D, 2, FF), D ** -0.5, 0.09375, ((0, 16), (1, 2)))
    w_out = noise(seeds[6], (EXPERTS, FF, D), FF ** -0.5, 0.1875, ((0, 16), (2, 2)))
    shared_in = noise(seeds[7], (D, 2, SFF), D ** -0.5, 0.09375, ((0, 2),))
    shared_out = noise(seeds[8], (SFF, D), SFF ** -0.5, 0.125, ((1, 2),))
    return {"tokens": tokens, "dest_device": dest_device, "local_slot": local_slot, "route_weights": route_weights, "copy_pick": copy_pick, "w_in": w_in, "w_out": w_out, "shared_in": shared_in, "shared_out": shared_out}


def blockwise(inputs, weights):
    width = D // N_DP
    total = jnp.zeros((inputs.shape[0], weights.shape[1]), jnp.float32)
    for block in range(N_DP):
        part = jnp.dot(inputs[:, block * width:(block + 1) * width], weights[block * width:(block + 1) * width], preferred_element_type=jnp.float32)
        part = lax.optimization_barrier(part.astype(jnp.bfloat16))
        total = total + part.astype(jnp.float32)
    return total


def reference(tokens, dest_device, local_slot, route_weights, copy_pick, w_in, w_out, shared_in, shared_out):
    tile_size = 16
    pick_total = ROWS * TOP
    device = dest_device.reshape(-1).astype(jnp.int32)
    slot_pick = local_slot.reshape(-1).astype(jnp.int32)
    replica = jnp.maximum(slot_pick - EXP_DEV, 0).astype(jnp.int32)
    source = jnp.mod(device - replica - 1, N_EXPERT).astype(jnp.int32)
    copied = (source * EXP_DEV + copy_pick[source, replica]).astype(jnp.int32)
    home_id = (device * EXP_DEV + jnp.minimum(slot_pick, EXP_DEV - 1)).astype(jnp.int32)
    expert = jnp.where(slot_pick < EXP_DEV, home_id, copied).astype(jnp.int32)
    onehot = (expert[:, None] == jnp.arange(EXPERTS, dtype=jnp.int32)[None, :]).astype(jnp.int32)
    counts = jnp.sum(onehot, axis=0).astype(jnp.int32)
    rounded = ((counts + tile_size - 1) // tile_size * tile_size).astype(jnp.int32)
    block_end = jnp.cumsum(rounded).astype(jnp.int32)
    block_start = (block_end - rounded).astype(jnp.int32)
    earlier = (jnp.cumsum(onehot, axis=0) - onehot).astype(jnp.int32)
    position = jnp.sum(earlier * onehot, axis=1).astype(jnp.int32)
    placed = (jnp.sum(block_start[None, :] * onehot, axis=1) + position).astype(jnp.int32)
    tile_count = (pick_total + tile_size - 1) // tile_size + EXPERTS
    row_of = (jnp.arange(pick_total, dtype=jnp.int32) // TOP).astype(jnp.int32)
    owners = jnp.full((tile_count * tile_size,), ROWS, jnp.int32).at[placed].set(row_of)
    tile_first = (jnp.arange(tile_count, dtype=jnp.int32) * tile_size).astype(jnp.int32)
    passed = jnp.sum((block_end[None, :] <= tile_first[:, None]).astype(jnp.int32), axis=1)
    tile_expert = jnp.minimum(passed, EXPERTS - 1).astype(jnp.int32)
    padded = jnp.concatenate([tokens, jnp.zeros((1, D), jnp.bfloat16)], axis=0)

    def expert_tile(args):
        tile_owners, which = args
        inputs = padded[tile_owners]
        gate_up = lax.dynamic_index_in_dim(w_in, which, 0, keepdims=False).reshape(D, 2 * FF)
        down_weight = lax.dynamic_index_in_dim(w_out, which, 0, keepdims=False)
        pre = blockwise(inputs, gate_up)
        hidden = (jax.nn.silu(pre[:, :FF]) * pre[:, FF:]).astype(jnp.bfloat16)
        return jnp.dot(hidden, down_weight, preferred_element_type=jnp.float32).astype(jnp.bfloat16)

    values = lax.map(expert_tile, (owners.reshape(tile_count, tile_size), tile_expert))
    picked = values.reshape(tile_count * tile_size, D)[placed].reshape(ROWS, TOP, D)
    norm_weight = route_weights / jnp.sum(route_weights, axis=1, keepdims=True)
    routed = jnp.sum(norm_weight[:, :, None] * picked.astype(jnp.float32), axis=1)
    shared_pre = blockwise(tokens, shared_in.reshape(D, 2 * SFF))
    shared_hidden = (jax.nn.silu(shared_pre[:, :SFF]) * shared_pre[:, SFF:]).astype(jnp.bfloat16)
    shared_value = jnp.dot(shared_hidden, shared_out, preferred_element_type=jnp.float32)
    return (shared_value + routed).astype(jnp.bfloat16)
```

```python
import functools
import jax
import jax.numpy as jnp
from jax import lax
from jax.experimental import pallas as pl
from jax.experimental.pallas import tpu as pltpu
from jax.sharding import PartitionSpec as P

LANE = 128
MESH = pl.DeviceIdType.MESH
F32 = jnp.float32
BF16 = jnp.bfloat16


def layer_kernel(
    dims, tokens, dest, slot, weights, pick, w_in, w_out, shared_in, shared_out, out,
    gathered, row_block, wide, scale, win_v, sin_v, wout_v, sout_v,
    part, part_in, spart, spart_in, hid, shid, acc, osend, orecv,
    win_sem, sin_sem, wout_sem, sout_sem, tok_s, tok_r, part_s, part_r, hid_s, hid_r,
    spart_s, spart_r, shid_s, shid_r, out_s, out_r,
):
    n_dp, groups, experts, copies, chunk, shared_active = dims
    rows_dev, depth = tokens.shape
    rows = rows_dev * groups
    mine = rows // n_dp
    per_expert = w_in.shape[3] // chunk
    chunks = experts * per_expert
    halves = chunk // LANE
    table = (gathered.shape[2] - depth) // 2
    slots = experts + copies
    me_dp, me = lax.axis_index("dp"), lax.axis_index("expert")

    def dp_at(step):
        return lax.rem(me_dp + step, n_dp)

    def dp_from(step):
        return lax.rem(me_dp + n_dp - step, n_dp)

    def group_at(step):
        return lax.rem(me + step, groups)

    def group_from(step):
        return lax.rem(me + groups - step, groups)

    shared_width = sin_v.shape[0] * LANE
    shared_blocks = shared_in.shape[2] // shared_width
    shared_at = pl.multiple_of(lax.rem(me, shared_blocks) * shared_width, LANE)

    def shared_in_copy(half):
        return pltpu.make_async_copy(
            shared_in.at[:, :, pl.ds(pl.multiple_of(shared_at + half * LANE, LANE), LANE)],
            sin_v.at[half], sin_sem.at[half])

    def win_copy(c, half):
        e, f = c // per_expert, lax.rem(c, per_expert)
        start = pl.multiple_of(f * chunk + half * LANE, LANE)
        return pltpu.make_async_copy(
            w_in.at[e, :, :, pl.ds(start, LANE)], win_v.at[c, half], win_sem.at[c, half])

    def wout_copy(c):
        e, f = c // per_expert, lax.rem(c, per_expert)
        start = pl.multiple_of(f * chunk, chunk)
        return pltpu.make_async_copy(
            w_out.at[e, pl.ds(start, chunk), :], wout_v.at[c], wout_sem.at[c])

    shared_out_copy = pltpu.make_async_copy(
        shared_out.at[pl.ds(shared_at, shared_width), :], sout_v, sout_sem)

    for half in range(sin_v.shape[0]):
        shared_in_copy(half).start()

    @pl.loop(0, chunks)
    def _(c):
        for half in range(halves):
            win_copy(c, half).start()

    shared_out_copy.start()

    @pl.loop(0, chunks)
    def _(c):
        wout_copy(c).start()

    barrier = pltpu.get_barrier_semaphore()

    @pl.loop(1, groups)
    def _(i):
        pl.semaphore_signal(
            barrier, inc=1, device_id=(me_dp, group_at(i)), device_id_type=MESH)

    @pl.loop(1, n_dp)
    def _(i):
        pl.semaphore_signal(barrier, inc=1, device_id=(dp_at(i), me), device_id_type=MESH)

    raw = weights[...]
    norm = raw / jnp.sum(raw, axis=1, keepdims=True)
    key = dest[...] * slots + slot[...]
    lanes = lax.broadcasted_iota(jnp.int32, (rows_dev, table), 1)
    spread = jnp.zeros((rows_dev, table), F32)
    for k in range(key.shape[1]):
        spread = spread + jnp.where(lanes == key[:, k:k + 1], norm[:, k:k + 1], 0.0)
    high = spread.astype(BF16)
    low = (spread - high.astype(F32)).astype(BF16)
    gathered[me] = jnp.concatenate([tokens[...], high, low], axis=1)

    pl.semaphore_wait(barrier, groups - 1 + n_dp - 1)

    def token_copy(i, block, target):
        return pltpu.make_async_remote_copy(
            src_ref=gathered.at[block], dst_ref=gathered.at[block],
            send_sem=tok_s.at[i], recv_sem=tok_r.at[i],
            device_id=(me_dp, target), device_id_type=MESH)

    @pl.loop(1, groups)
    def _(i):
        token_copy(i, me, group_at(i)).start()

    at_row = lax.broadcasted_iota(jnp.int32, (LANE, 4 * LANE), 0)
    at_col = lax.broadcasted_iota(jnp.int32, (LANE, 4 * LANE), 1)
    goal = jnp.where(at_col < 2 * LANE, 2 * at_row, 2 * at_row + 1 + 2 * LANE)
    spreader = jnp.where(at_col == goal, 1.0, 0.0).astype(BF16)

    @pl.loop(1, groups)
    def _(i):
        token_copy(i, group_from(i), group_from(i)).wait_recv()

    for q in range(groups):
        row_block[q * rows_dev:(q + 1) * rows_dev, :] = gathered[q].astype(F32)

    for b in range(depth // LANE):
        block = row_block[:, b * LANE:(b + 1) * LANE].astype(BF16)
        both = jnp.dot(block, spreader, preferred_element_type=F32).astype(BF16)
        wide[0:rows, 2 * b * LANE:2 * (b + 1) * LANE] = both[:, :2 * LANE]
        wide[rows:, 2 * b * LANE:2 * (b + 1) * LANE] = both[:, 2 * LANE:]

    total = row_block[:, depth:depth + table] + row_block[:, depth + table:]
    lanes = lax.broadcasted_iota(jnp.int32, (rows, table), 1)
    for e in range(experts):
        keep = jnp.where(lanes == me * slots + e, 1.0, 0.0)
        for r in range(copies):
            taken = jnp.where(pick[0, r] == e, 1.0, 0.0)
            at = lax.rem(me + r + 1, groups) * slots + experts + r
            keep = keep + jnp.where(lanes == at, taken, 0.0)
        value = jnp.sum(total * keep, axis=1, keepdims=True)
        scale[e] = jnp.broadcast_to(value, (rows, LANE))

    def part_copy(c, i, source, target):
        return pltpu.make_async_remote_copy(
            src_ref=part.at[c, target], dst_ref=part_in.at[c, source],
            send_sem=part_s.at[c, i], recv_sem=part_r.at[c, i],
            device_id=(target, me), device_id_type=MESH)

    def hid_copy(c, i, source, target):
        return pltpu.make_async_remote_copy(
            src_ref=hid.at[c, source], dst_ref=hid.at[c, source],
            send_sem=hid_s.at[c, i], recv_sem=hid_r.at[c, i],
            device_id=(target, me), device_id_type=MESH)

    def spart_copy(i, source, target):
        return pltpu.make_async_remote_copy(
            src_ref=spart.at[target], dst_ref=spart_in.at[source],
            send_sem=spart_s.at[i], recv_sem=spart_r.at[i],
            device_id=(target, me), device_id_type=MESH)

    def shid_copy(i, source, target):
        return pltpu.make_async_remote_copy(
            src_ref=shid.at[source], dst_ref=shid.at[source],
            send_sem=shid_s.at[i], recv_sem=shid_r.at[i],
            device_id=(target, me), device_id_type=MESH)

    def flat(ref):
        return ref.reshape(2 * depth, LANE)[...]

    def project(blocks):
        matrix = blocks[0] if len(blocks) == 1 else jnp.concatenate(blocks, axis=1)
        value = jnp.dot(wide[...], matrix, preferred_element_type=F32)
        return value.astype(BF16).reshape(2, n_dp, mine, matrix.shape[1])

    def activated(total):
        gate, up = total[0], total[1]
        return gate / (1.0 + jnp.exp(-gate)) * up

    for half in range(sin_v.shape[0]):
        shared_in_copy(half).wait()
    value = project([flat(sin_v.at[half]) for half in range(sin_v.shape[0])])
    for p in range(n_dp):
        spart[p] = value[:, p]

    @pl.loop(1, n_dp)
    def _(i):
        spart_copy(i, me_dp, dp_at(i)).start()

    def first(c):
        for half in range(halves):
            win_copy(c, half).wait()
        value = project([flat(win_v.at[c, half]) for half in range(halves)])
        for p in range(n_dp):
            part[c, p] = value[:, p]

        @pl.loop(1, n_dp)
        def _(i):
            part_copy(c, i, me_dp, dp_at(i)).start()

    def middle(c):
        total = part[c, me_dp].astype(F32)
        for i in range(1, n_dp):
            part_copy(c, i, dp_from(i), me_dp).wait_recv()
            total = total + part_in[c, dp_from(i)].astype(F32)
        factor = scale[c // per_expert, pl.ds(pl.multiple_of(me_dp * mine, mine), mine), :]
        hid[c, me_dp] = (activated(total) * factor[:, :1]).astype(BF16)

        @pl.loop(1, n_dp)
        def _(i):
            hid_copy(c, i, me_dp, dp_at(i)).start()

    def shared_middle():
        total = spart[me_dp].astype(F32)
        for i in range(1, n_dp):
            spart_copy(i, dp_from(i), me_dp).wait_recv()
            total = total + spart_in[dp_from(i)].astype(F32)
        active = jnp.where(me < shared_active, 1.0, 0.0)
        shid[me_dp] = (activated(total) * active).astype(BF16)

        @pl.loop(1, n_dp)
        def _(i):
            shid_copy(i, me_dp, dp_at(i)).start()

    def last(c):
        for i in range(1, n_dp):
            hid_copy(c, i, dp_from(i), me_dp).wait_recv()
        wout_copy(c).wait()
        acc[...] += jnp.dot(
            hid[c].reshape(rows, chunk), wout_v[c], preferred_element_type=F32)

    def shared_last():
        for i in range(1, n_dp):
            shid_copy(i, dp_from(i), me_dp).wait_recv()
        shared_out_copy.wait()
        acc[...] = jnp.dot(
            shid[...].reshape(rows, shared_width), sout_v[...], preferred_element_type=F32)

    lag = 3

    @pl.loop(0, chunks + lag)
    def _(c):
        @pl.when(c < chunks)
        def _():
            first(c)

        @pl.when(c == 0)
        def _():
            shared_middle()

        @pl.when((c >= 1) & (c <= chunks))
        def _():
            middle(c - 1)

        @pl.when(c == lag - 1)
        def _():
            shared_last()

        @pl.when(c >= lag)
        def _():
            last(c - lag)

    def out_copy(i, source, target):
        return pltpu.make_async_remote_copy(
            src_ref=osend.at[target], dst_ref=orecv.at[source],
            send_sem=out_s.at[i], recv_sem=out_r.at[i],
            device_id=(me_dp, target), device_id_type=MESH)

    for q in range(groups):
        osend[q] = acc[q * rows_dev:(q + 1) * rows_dev, :].astype(BF16)

    @pl.loop(1, groups)
    def _(i):
        out_copy(i, me, group_at(i)).start()

    orecv[me] = osend[me]

    @pl.loop(1, groups)
    def _(i):
        token_copy(i, me, group_at(i)).wait_send()

    @pl.loop(1, n_dp)
    def _(i):
        spart_copy(i, me_dp, dp_at(i)).wait_send()
        shid_copy(i, me_dp, dp_at(i)).wait_send()

        @pl.loop(0, chunks)
        def _(c):
            part_copy(c, i, me_dp, dp_at(i)).wait_send()
            hid_copy(c, i, me_dp, dp_at(i)).wait_send()

    @pl.loop(1, groups)
    def _(i):
        out_copy(i, group_from(i), me).wait_recv()

    total = orecv[0].astype(F32)
    for q in range(1, groups):
        total = total + orecv[q].astype(F32)
    out[...] = total.astype(BF16)

    @pl.loop(1, groups)
    def _(i):
        out_copy(i, me, group_at(i)).wait_send()


def per_device(
    tokens, dest_device, local_slot, route_weights, copy_pick, w_in, w_out, shared_in, shared_out
):
    n_dp, groups = lax.axis_size("dp"), lax.axis_size("expert")
    rows_dev, depth = tokens.shape
    experts, _, _, units = w_in.shape
    copies = copy_pick.shape[1]
    shared_units = shared_in.shape[2]
    rows = rows_dev * groups
    mine = rows // n_dp
    chunk = 2 * LANE
    chunks = experts * units // chunk
    table = -(-groups * (experts + copies) // LANE) * LANE
    shared_blocks = max(1, shared_units // (LANE * groups))
    shared_width = shared_blocks * LANE
    shared_active = shared_units // shared_width
    vmem = pl.BlockSpec(memory_space=pltpu.VMEM)
    hbm = pl.BlockSpec(memory_space=pl.ANY)
    dma = pltpu.SemaphoreType.DMA
    dims = (n_dp, groups, experts, copies, chunk, shared_active)
    return pl.pallas_call(
        functools.partial(layer_kernel, dims),
        out_shape=jax.ShapeDtypeStruct((rows_dev, depth), BF16),
        in_specs=[vmem] * 4 + [pl.BlockSpec(memory_space=pltpu.SMEM)] + [hbm] * 4,
        out_specs=vmem,
        scratch_shapes=[
            pltpu.VMEM((groups, rows_dev, depth + 2 * table), BF16),
            pltpu.VMEM((rows, depth + 2 * table), F32),
            pltpu.VMEM((2 * rows, 2 * depth), BF16),
            pltpu.VMEM((experts, rows, LANE), F32),
            pltpu.VMEM((chunks, chunk // LANE, depth, 2, LANE), BF16),
            pltpu.VMEM((shared_blocks, depth, 2, LANE), BF16),
            pltpu.VMEM((chunks, chunk, depth), BF16),
            pltpu.VMEM((shared_width, depth), BF16),
            pltpu.VMEM((chunks, n_dp, 2, mine, chunk), BF16),
            pltpu.VMEM((chunks, n_dp, 2, mine, chunk), BF16),
            pltpu.VMEM((n_dp, 2, mine, shared_width), BF16),
            pltpu.VMEM((n_dp, 2, mine, shared_width), BF16),
            pltpu.VMEM((chunks, n_dp, mine, chunk), BF16),
            pltpu.VMEM((n_dp, mine, shared_width), BF16),
            pltpu.VMEM((rows, depth), F32),
            pltpu.VMEM((groups, rows_dev, depth), BF16),
            pltpu.VMEM((groups, rows_dev, depth), BF16),
            dma((chunks, chunk // LANE)),
            dma((shared_blocks,)),
            dma((chunks,)),
            dma,
            dma((groups,)),
            dma((groups,)),
            dma((chunks, n_dp)),
            dma((chunks, n_dp)),
            dma((chunks, n_dp)),
            dma((chunks, n_dp)),
            dma((n_dp,)),
            dma((n_dp,)),
            dma((n_dp,)),
            dma((n_dp,)),
            dma((groups,)),
            dma((groups,)),
        ],
        compiler_params=pltpu.CompilerParams(
            collective_id=0, has_side_effects=True, vmem_limit_bytes=56 * 1024 * 1024
        ),
    )(tokens, dest_device, local_slot, route_weights, copy_pick, w_in, w_out, shared_in, shared_out)


def solution(mesh):
    in_specs = (
        P("expert", "dp"),
        P("expert", None),
        P("expert", None),
        P("expert", None),
        P("expert", None),
        P("expert", "dp", None, None),
        P("expert", None, "dp"),
        P("dp", None, None),
        P(None, "dp"),
    )
    out_specs = P("expert", "dp")
    return jax.shard_map(
        per_device, mesh=mesh, in_specs=in_specs, out_specs=out_specs, check_vma=False
    )
```

```python
import functools
import jax
import jax.numpy as jnp
from jax import lax
from jax.experimental import pallas as pl
from jax.experimental.pallas import tpu as pltpu
from jax.sharding import PartitionSpec as P

LANE = 128
MESH = pl.DeviceIdType.MESH
F32 = jnp.float32
BF16 = jnp.bfloat16


def layer_kernel(
    dims, tokens, dest, slot, weights, pick, w_in, w_out, shared_in, shared_out, out,
    gathered, row_block, wide, scale, win_v, sin_v, wout_v, sout_v,
    part, part_in, spart, spart_in, hid, shid, acc, osend, orecv,
    win_sem, sin_sem, wout_sem, sout_sem, tok_s, tok_r, part_s, part_r, hid_s, hid_r,
    spart_s, spart_r, shid_s, shid_r, out_s, out_r,
):
    n_dp, groups, experts, copies, chunk, shared_active = dims
    rows_dev, depth = tokens.shape
    rows = rows_dev * groups
    mine = rows // n_dp
    per_expert = w_in.shape[3] // chunk
    chunks = experts * per_expert
    units = w_in.shape[3]
    table = (gathered.shape[2] - depth) // 2
    slots = experts + copies
    me_dp, me = lax.axis_index("dp"), lax.axis_index("expert")

    def dp_at(step):
        return lax.rem(me_dp + step, n_dp)

    def dp_from(step):
        return lax.rem(me_dp + n_dp - step, n_dp)

    def group_at(step):
        return lax.rem(me + step, groups)

    def group_from(step):
        return lax.rem(me + groups - step, groups)

    shared_width = sin_v.shape[0] * LANE
    shared_blocks = shared_in.shape[2] // shared_width
    shared_at = pl.multiple_of(lax.rem(me, shared_blocks) * shared_width, LANE)

    def shared_in_copy(half):
        return pltpu.make_async_copy(
            shared_in.at[:, :, pl.ds(pl.multiple_of(shared_at + half * LANE, LANE), LANE)],
            sin_v.at[half], sin_sem.at[half])

    def win_copy(e):
        return pltpu.make_async_copy(w_in.at[e], win_v.at[e], win_sem.at[e])

    def wout_copy(c):
        e, f = c // per_expert, lax.rem(c, per_expert)
        start = pl.multiple_of(f * chunk, chunk)
        return pltpu.make_async_copy(
            w_out.at[e, pl.ds(start, chunk), :], wout_v.at[c], wout_sem.at[c])

    shared_out_copy = pltpu.make_async_copy(
        shared_out.at[pl.ds(shared_at, shared_width), :], sout_v, sout_sem)

    for half in range(sin_v.shape[0]):
        shared_in_copy(half).start()

    @pl.loop(0, experts)
    def _(e):
        win_copy(e).start()

    shared_out_copy.start()

    @pl.loop(0, chunks)
    def _(c):
        wout_copy(c).start()

    barrier = pltpu.get_barrier_semaphore()

    @pl.loop(1, groups)
    def _(i):
        pl.semaphore_signal(
            barrier, inc=1, device_id=(me_dp, group_at(i)), device_id_type=MESH)

    @pl.loop(1, n_dp)
    def _(i):
        pl.semaphore_signal(barrier, inc=1, device_id=(dp_at(i), me), device_id_type=MESH)

    raw = weights[...]
    norm = raw / jnp.sum(raw, axis=1, keepdims=True)
    key = dest[...] * slots + slot[...]
    lanes = lax.broadcasted_iota(jnp.int32, (rows_dev, table), 1)
    spread = jnp.zeros((rows_dev, table), F32)
    for k in range(key.shape[1]):
        spread = spread + jnp.where(lanes == key[:, k:k + 1], norm[:, k:k + 1], 0.0)
    high = spread.astype(BF16)
    low = (spread - high.astype(F32)).astype(BF16)
    gathered[me] = jnp.concatenate([tokens[...], high, low], axis=1)

    pl.semaphore_wait(barrier, groups - 1 + n_dp - 1)

    def token_copy(i, block, target):
        return pltpu.make_async_remote_copy(
            src_ref=gathered.at[block], dst_ref=gathered.at[block],
            send_sem=tok_s.at[i], recv_sem=tok_r.at[i],
            device_id=(me_dp, target), device_id_type=MESH)

    @pl.loop(1, groups)
    def _(i):
        token_copy(i, me, group_at(i)).start()

    at_row = lax.broadcasted_iota(jnp.int32, (LANE, 4 * LANE), 0)
    at_col = lax.broadcasted_iota(jnp.int32, (LANE, 4 * LANE), 1)
    goal = jnp.where(at_col < 2 * LANE, 2 * at_row, 2 * at_row + 1 + 2 * LANE)
    spreader = jnp.where(at_col == goal, 1.0, 0.0).astype(BF16)

    @pl.loop(1, groups)
    def _(i):
        token_copy(i, group_from(i), group_from(i)).wait_recv()

    for q in range(groups):
        row_block[q * rows_dev:(q + 1) * rows_dev, :] = gathered[q].astype(F32)

    for b in range(depth // LANE):
        block = row_block[:, b * LANE:(b + 1) * LANE].astype(BF16)
        both = jnp.dot(block, spreader, preferred_element_type=F32).astype(BF16)
        wide[0:rows, 2 * b * LANE:2 * (b + 1) * LANE] = both[:, :2 * LANE]
        wide[rows:, 2 * b * LANE:2 * (b + 1) * LANE] = both[:, 2 * LANE:]

    total = row_block[:, depth:depth + table] + row_block[:, depth + table:]
    lanes = lax.broadcasted_iota(jnp.int32, (rows, table), 1)
    for e in range(experts):
        keep = jnp.where(lanes == me * slots + e, 1.0, 0.0)
        for r in range(copies):
            taken = jnp.where(pick[0, r] == e, 1.0, 0.0)
            at = lax.rem(me + r + 1, groups) * slots + experts + r
            keep = keep + jnp.where(lanes == at, taken, 0.0)
        value = jnp.sum(total * keep, axis=1, keepdims=True)
        scale[e] = jnp.broadcast_to(value, (rows, LANE))

    def part_copy(c, i, source, target):
        return pltpu.make_async_remote_copy(
            src_ref=part.at[c, target], dst_ref=part_in.at[c, source],
            send_sem=part_s.at[c, i], recv_sem=part_r.at[c, i],
            device_id=(target, me), device_id_type=MESH)

    def hid_copy(c, i, source, target):
        return pltpu.make_async_remote_copy(
            src_ref=hid.at[c, source], dst_ref=hid.at[c, source],
            send_sem=hid_s.at[c, i], recv_sem=hid_r.at[c, i],
            device_id=(target, me), device_id_type=MESH)

    def spart_copy(i, source, target):
        return pltpu.make_async_remote_copy(
            src_ref=spart.at[target], dst_ref=spart_in.at[source],
            send_sem=spart_s.at[i], recv_sem=spart_r.at[i],
            device_id=(target, me), device_id_type=MESH)

    def shid_copy(i, source, target):
        return pltpu.make_async_remote_copy(
            src_ref=shid.at[source], dst_ref=shid.at[source],
            send_sem=shid_s.at[i], recv_sem=shid_r.at[i],
            device_id=(target, me), device_id_type=MESH)

    def flat(ref):
        return ref.reshape(2 * depth, LANE)[...]

    def project(blocks):
        matrix = blocks[0] if len(blocks) == 1 else jnp.concatenate(blocks, axis=1)
        value = jnp.dot(wide[...], matrix, preferred_element_type=F32)
        return value.astype(BF16).reshape(2, n_dp, mine, matrix.shape[1])

    def activated(total):
        gate, up = total[0], total[1]
        return gate / (1.0 + jnp.exp(-gate)) * up

    for half in range(sin_v.shape[0]):
        shared_in_copy(half).wait()
    value = project([flat(sin_v.at[half]) for half in range(sin_v.shape[0])])
    for p in range(n_dp):
        spart[p] = value[:, p]

    @pl.loop(1, n_dp)
    def _(i):
        spart_copy(i, me_dp, dp_at(i)).start()

    def first(c):
        e, f = c // per_expert, lax.rem(c, per_expert)

        @pl.when(f == 0)
        def _():
            win_copy(e).wait()

        start = pl.multiple_of(f * chunk, chunk)
        value = project([win_v.at[e].reshape(2 * depth, units)[:, pl.ds(start, chunk)]])
        for p in range(n_dp):
            part[c, p] = value[:, p]

        @pl.loop(1, n_dp)
        def _(i):
            part_copy(c, i, me_dp, dp_at(i)).start()

    def middle(c):
        total = part[c, me_dp].astype(F32)
        for i in range(1, n_dp):
            part_copy(c, i, dp_from(i), me_dp).wait_recv()
            total = total + part_in[c, dp_from(i)].astype(F32)
        factor = scale[c // per_expert, pl.ds(pl.multiple_of(me_dp * mine, mine), mine), :]
        hid[c, me_dp] = (activated(total) * factor[:, :1]).astype(BF16)

        @pl.loop(1, n_dp)
        def _(i):
            hid_copy(c, i, me_dp, dp_at(i)).start()

    def shared_middle():
        total = spart[me_dp].astype(F32)
        for i in range(1, n_dp):
            spart_copy(i, dp_from(i), me_dp).wait_recv()
            total = total + spart_in[dp_from(i)].astype(F32)
        active = jnp.where(me < shared_active, 1.0, 0.0)
        shid[me_dp] = (activated(total) * active).astype(BF16)

        @pl.loop(1, n_dp)
        def _(i):
            shid_copy(i, me_dp, dp_at(i)).start()

    def last(c):
        for i in range(1, n_dp):
            hid_copy(c, i, dp_from(i), me_dp).wait_recv()
        wout_copy(c).wait()
        acc[...] += jnp.dot(
            hid[c].reshape(rows, chunk), wout_v[c], preferred_element_type=F32)

    def shared_last():
        for i in range(1, n_dp):
            shid_copy(i, dp_from(i), me_dp).wait_recv()
        shared_out_copy.wait()
        acc[...] = jnp.dot(
            shid[...].reshape(rows, shared_width), sout_v[...], preferred_element_type=F32)

    lag = 3

    @pl.loop(0, chunks + lag)
    def _(c):
        @pl.when(c < chunks)
        def _():
            first(c)

        @pl.when(c == 0)
        def _():
            shared_middle()

        @pl.when((c >= 1) & (c <= chunks))
        def _():
            middle(c - 1)

        @pl.when(c == lag - 1)
        def _():
            shared_last()

        @pl.when(c >= lag)
        def _():
            last(c - lag)

    def out_copy(i, source, target):
        return pltpu.make_async_remote_copy(
            src_ref=osend.at[target], dst_ref=orecv.at[source],
            send_sem=out_s.at[i], recv_sem=out_r.at[i],
            device_id=(me_dp, target), device_id_type=MESH)

    for q in range(groups):
        osend[q] = acc[q * rows_dev:(q + 1) * rows_dev, :].astype(BF16)

    @pl.loop(1, groups)
    def _(i):
        out_copy(i, me, group_at(i)).start()

    orecv[me] = osend[me]

    @pl.loop(1, groups)
    def _(i):
        token_copy(i, me, group_at(i)).wait_send()

    @pl.loop(1, n_dp)
    def _(i):
        spart_copy(i, me_dp, dp_at(i)).wait_send()
        shid_copy(i, me_dp, dp_at(i)).wait_send()

        @pl.loop(0, chunks)
        def _(c):
            part_copy(c, i, me_dp, dp_at(i)).wait_send()
            hid_copy(c, i, me_dp, dp_at(i)).wait_send()

    @pl.loop(1, groups)
    def _(i):
        out_copy(i, group_from(i), me).wait_recv()

    total = orecv[0].astype(F32)
    for q in range(1, groups):
        total = total + orecv[q].astype(F32)
    out[...] = total.astype(BF16)

    @pl.loop(1, groups)
    def _(i):
        out_copy(i, me, group_at(i)).wait_send()


def per_device(
    tokens, dest_device, local_slot, route_weights, copy_pick, w_in, w_out, shared_in, shared_out
):
    n_dp, groups = lax.axis_size("dp"), lax.axis_size("expert")
    rows_dev, depth = tokens.shape
    experts, _, _, units = w_in.shape
    copies = copy_pick.shape[1]
    shared_units = shared_in.shape[2]
    rows = rows_dev * groups
    mine = rows // n_dp
    chunk = 2 * LANE
    chunks = experts * units // chunk
    table = -(-groups * (experts + copies) // LANE) * LANE
    shared_blocks = max(1, shared_units // (LANE * groups))
    shared_width = shared_blocks * LANE
    shared_active = shared_units // shared_width
    vmem = pl.BlockSpec(memory_space=pltpu.VMEM)
    hbm = pl.BlockSpec(memory_space=pl.ANY)
    dma = pltpu.SemaphoreType.DMA
    dims = (n_dp, groups, experts, copies, chunk, shared_active)
    return pl.pallas_call(
        functools.partial(layer_kernel, dims),
        out_shape=jax.ShapeDtypeStruct((rows_dev, depth), BF16),
        in_specs=[vmem] * 4 + [pl.BlockSpec(memory_space=pltpu.SMEM)] + [hbm] * 4,
        out_specs=vmem,
        scratch_shapes=[
            pltpu.VMEM((groups, rows_dev, depth + 2 * table), BF16),
            pltpu.VMEM((rows, depth + 2 * table), F32),
            pltpu.VMEM((2 * rows, 2 * depth), BF16),
            pltpu.VMEM((experts, rows, LANE), F32),
            pltpu.VMEM((experts, depth, 2, units), BF16),
            pltpu.VMEM((shared_blocks, depth, 2, LANE), BF16),
            pltpu.VMEM((chunks, chunk, depth), BF16),
            pltpu.VMEM((shared_width, depth), BF16),
            pltpu.VMEM((chunks, n_dp, 2, mine, chunk), BF16),
            pltpu.VMEM((chunks, n_dp, 2, mine, chunk), BF16),
            pltpu.VMEM((n_dp, 2, mine, shared_width), BF16),
            pltpu.VMEM((n_dp, 2, mine, shared_width), BF16),
            pltpu.VMEM((chunks, n_dp, mine, chunk), BF16),
            pltpu.VMEM((n_dp, mine, shared_width), BF16),
            pltpu.VMEM((rows, depth), F32),
            pltpu.VMEM((groups, rows_dev, depth), BF16),
            pltpu.VMEM((groups, rows_dev, depth), BF16),
            dma((experts,)),
            dma((shared_blocks,)),
            dma((chunks,)),
            dma,
            dma((groups,)),
            dma((groups,)),
            dma((chunks, n_dp)),
            dma((chunks, n_dp)),
            dma((chunks, n_dp)),
            dma((chunks, n_dp)),
            dma((n_dp,)),
            dma((n_dp,)),
            dma((n_dp,)),
            dma((n_dp,)),
            dma((groups,)),
            dma((groups,)),
        ],
        compiler_params=pltpu.CompilerParams(
            collective_id=0, has_side_effects=True, vmem_limit_bytes=56 * 1024 * 1024
        ),
    )(tokens, dest_device, local_slot, route_weights, copy_pick, w_in, w_out, shared_in, shared_out)


def solution(mesh):
    in_specs = (
        P("expert", "dp"),
        P("expert", None),
        P("expert", None),
        P("expert", None),
        P("expert", None),
        P("expert", "dp", None, None),
        P("expert", None, "dp"),
        P("dp", None, None),
        P(None, "dp"),
    )
    out_specs = P("expert", "dp")
    return jax.shard_map(
        per_device, mesh=mesh, in_specs=in_specs, out_specs=out_specs, check_vma=False
    )
```

```python
import functools
import jax
import jax.numpy as jnp
from jax import lax
from jax.experimental import pallas as pl
from jax.experimental.pallas import tpu as pltpu
from jax.sharding import PartitionSpec as P

LANE = 128
MESH = pl.DeviceIdType.MESH
F32 = jnp.float32
BF16 = jnp.bfloat16


def layer_kernel(
    dims, tokens, dest, slot, weights, pick, w_in, w_out, shared_in, shared_out, out,
    gathered, row_block, wide, scale, win_v, sin_v, wout_v, sout_v,
    part, part_in, spart, spart_in, hid, shid, acc, osend, opair, osum, orecv,
    win_sem, sin_sem, wout_sem, sout_sem, tok_s, tok_r, pass_s, pass_r, part_s, part_r, hid_s, hid_r,
    spart_s, spart_r, shid_s, shid_r, pair_s, pair_r, out_s, out_r,
):
    n_dp, groups, experts, copies, chunk, shared_active = dims
    rows_dev, depth = tokens.shape
    rows = rows_dev * groups
    mine = rows // n_dp
    per_expert = w_in.shape[3] // chunk
    chunks = experts * per_expert
    units = w_in.shape[3]
    table = (gathered.shape[2] - depth) // 2
    slots = experts + copies
    me_dp, me = lax.axis_index("dp"), lax.axis_index("expert")

    def dp_at(step):
        return lax.rem(me_dp + step, n_dp)

    def dp_from(step):
        return lax.rem(me_dp + n_dp - step, n_dp)

    chips = groups // 2
    core = lax.rem(me, 2)
    chip = me // 2
    sibling = 2 * chip + 1 - core

    def chip_at(step):
        return lax.rem(chip + step, chips)

    def chip_from(step):
        return lax.rem(chip + chips - step, chips)

    shared_width = sin_v.shape[0] * LANE
    shared_blocks = shared_in.shape[2] // shared_width
    shared_at = pl.multiple_of(lax.rem(me, shared_blocks) * shared_width, LANE)

    def shared_in_copy(half):
        return pltpu.make_async_copy(
            shared_in.at[:, :, pl.ds(pl.multiple_of(shared_at + half * LANE, LANE), LANE)],
            sin_v.at[half], sin_sem.at[half])

    def win_copy(e):
        return pltpu.make_async_copy(w_in.at[e], win_v.at[e], win_sem.at[e])

    def wout_copy(c):
        e, f = c // per_expert, lax.rem(c, per_expert)
        start = pl.multiple_of(f * chunk, chunk)
        return pltpu.make_async_copy(
            w_out.at[e, pl.ds(start, chunk), :], wout_v.at[c], wout_sem.at[c])

    shared_out_copy = pltpu.make_async_copy(
        shared_out.at[pl.ds(shared_at, shared_width), :], sout_v, sout_sem)

    for half in range(sin_v.shape[0]):
        shared_in_copy(half).start()

    win_copy(0).start()

    barrier = pltpu.get_barrier_semaphore()

    pl.semaphore_signal(barrier, inc=1, device_id=(me_dp, sibling), device_id_type=MESH)

    @pl.loop(1, chips)
    def _(i):
        pl.semaphore_signal(
            barrier, inc=1, device_id=(me_dp, 2 * chip_at(i) + core), device_id_type=MESH)

    @pl.loop(1, n_dp)
    def _(i):
        pl.semaphore_signal(barrier, inc=1, device_id=(dp_at(i), me), device_id_type=MESH)

    raw = weights[...]
    norm = raw / jnp.sum(raw, axis=1, keepdims=True)
    key = dest[...] * slots + slot[...]
    lanes = lax.broadcasted_iota(jnp.int32, (rows_dev, table), 1)
    spread = jnp.zeros((rows_dev, table), F32)
    for k in range(key.shape[1]):
        spread = spread + jnp.where(lanes == key[:, k:k + 1], norm[:, k:k + 1], 0.0)
    high = spread.astype(BF16)
    low = (spread - high.astype(F32)).astype(BF16)
    gathered[me] = jnp.concatenate([tokens[...], high, low], axis=1)

    pl.semaphore_wait(barrier, chips + n_dp - 1)

    def token_copy(i, block, target):
        return pltpu.make_async_remote_copy(
            src_ref=gathered.at[block], dst_ref=gathered.at[block],
            send_sem=tok_s.at[i], recv_sem=tok_r.at[i],
            device_id=(me_dp, target), device_id_type=MESH)

    def pass_copy(i, block):
        return pltpu.make_async_remote_copy(
            src_ref=gathered.at[block], dst_ref=gathered.at[block],
            send_sem=pass_s.at[i], recv_sem=pass_r.at[i],
            device_id=(me_dp, sibling), device_id_type=MESH)

    @pl.loop(1, chips)
    def _(i):
        token_copy(i, me, 2 * chip_at(i) + core).start()

    pass_copy(0, me).start()

    @pl.loop(1, experts)
    def _(e):
        win_copy(e).start()

    shared_out_copy.start()

    @pl.loop(0, chunks)
    def _(c):
        wout_copy(c).start()

    at_row = lax.broadcasted_iota(jnp.int32, (LANE, 4 * LANE), 0)
    at_col = lax.broadcasted_iota(jnp.int32, (LANE, 4 * LANE), 1)
    goal = jnp.where(at_col < 2 * LANE, 2 * at_row, 2 * at_row + 1 + 2 * LANE)
    spreader = jnp.where(at_col == goal, 1.0, 0.0).astype(BF16)

    @pl.loop(1, chips)
    def _(i):
        block = 2 * chip_from(i) + core
        token_copy(i, block, me).wait_recv()
        pass_copy(i, block).start()

    @pl.loop(0, chips)
    def _(i):
        pass_copy(i, 2 * chip_from(i) + 1 - core).wait_recv()

    for q in range(groups):
        row_block[q * rows_dev:(q + 1) * rows_dev, :] = gathered[q].astype(F32)

    for b in range(depth // LANE):
        block = row_block[:, b * LANE:(b + 1) * LANE].astype(BF16)
        both = jnp.dot(block, spreader, preferred_element_type=F32).astype(BF16)
        wide[0:rows, 2 * b * LANE:2 * (b + 1) * LANE] = both[:, :2 * LANE]
        wide[rows:, 2 * b * LANE:2 * (b + 1) * LANE] = both[:, 2 * LANE:]

    total = row_block[:, depth:depth + table] + row_block[:, depth + table:]
    lanes = lax.broadcasted_iota(jnp.int32, (rows, table), 1)
    for e in range(experts):
        keep = jnp.where(lanes == me * slots + e, 1.0, 0.0)
        for r in range(copies):
            taken = jnp.where(pick[0, r] == e, 1.0, 0.0)
            at = lax.rem(me + r + 1, groups) * slots + experts + r
            keep = keep + jnp.where(lanes == at, taken, 0.0)
        value = jnp.sum(total * keep, axis=1, keepdims=True)
        scale[e] = jnp.broadcast_to(value, (rows, LANE))

    def part_copy(c, i, source, target):
        return pltpu.make_async_remote_copy(
            src_ref=part.at[c, target], dst_ref=part_in.at[c, source],
            send_sem=part_s.at[c, i], recv_sem=part_r.at[c, i],
            device_id=(target, me), device_id_type=MESH)

    def hid_copy(c, i, source, target):
        return pltpu.make_async_remote_copy(
            src_ref=hid.at[c, source], dst_ref=hid.at[c, source],
            send_sem=hid_s.at[c, i], recv_sem=hid_r.at[c, i],
            device_id=(target, me), device_id_type=MESH)

    def spart_copy(i, source, target):
        return pltpu.make_async_remote_copy(
            src_ref=spart.at[target], dst_ref=spart_in.at[source],
            send_sem=spart_s.at[i], recv_sem=spart_r.at[i],
            device_id=(target, me), device_id_type=MESH)

    def shid_copy(i, source, target):
        return pltpu.make_async_remote_copy(
            src_ref=shid.at[source], dst_ref=shid.at[source],
            send_sem=shid_s.at[i], recv_sem=shid_r.at[i],
            device_id=(target, me), device_id_type=MESH)

    def flat(ref):
        return ref.reshape(2 * depth, LANE)[...]

    def project(blocks):
        matrix = blocks[0] if len(blocks) == 1 else jnp.concatenate(blocks, axis=1)
        value = jnp.dot(wide[...], matrix, preferred_element_type=F32)
        return value.astype(BF16).reshape(2, n_dp, mine, matrix.shape[1])

    def activated(total):
        gate, up = total[0], total[1]
        return gate / (1.0 + jnp.exp(-gate)) * up

    for half in range(sin_v.shape[0]):
        shared_in_copy(half).wait()
    value = project([flat(sin_v.at[half]) for half in range(sin_v.shape[0])])
    for p in range(n_dp):
        spart[p] = value[:, p]

    @pl.loop(1, n_dp)
    def _(i):
        spart_copy(i, me_dp, dp_at(i)).start()

    def first(c):
        e, f = c // per_expert, lax.rem(c, per_expert)

        @pl.when(f == 0)
        def _():
            win_copy(e).wait()

        start = pl.multiple_of(f * chunk, chunk)
        value = project([win_v.at[e].reshape(2 * depth, units)[:, pl.ds(start, chunk)]])
        for p in range(n_dp):
            part[c, p] = value[:, p]

        @pl.loop(1, n_dp)
        def _(i):
            part_copy(c, i, me_dp, dp_at(i)).start()

    def middle(c):
        total = part[c, me_dp].astype(F32)
        for i in range(1, n_dp):
            part_copy(c, i, dp_from(i), me_dp).wait_recv()
            total = total + part_in[c, dp_from(i)].astype(F32)
        factor = scale[c // per_expert, pl.ds(pl.multiple_of(me_dp * mine, mine), mine), :]
        hid[c, me_dp] = (activated(total) * factor[:, :1]).astype(BF16)

        @pl.loop(1, n_dp)
        def _(i):
            hid_copy(c, i, me_dp, dp_at(i)).start()

    def shared_middle():
        total = spart[me_dp].astype(F32)
        for i in range(1, n_dp):
            spart_copy(i, dp_from(i), me_dp).wait_recv()
            total = total + spart_in[dp_from(i)].astype(F32)
        active = jnp.where(me < shared_active, 1.0, 0.0)
        shid[me_dp] = (activated(total) * active).astype(BF16)

        @pl.loop(1, n_dp)
        def _(i):
            shid_copy(i, me_dp, dp_at(i)).start()

    def last(c):
        for i in range(1, n_dp):
            hid_copy(c, i, dp_from(i), me_dp).wait_recv()
        wout_copy(c).wait()
        acc[...] += jnp.dot(
            hid[c].reshape(rows, chunk), wout_v[c], preferred_element_type=F32)

    def shared_last():
        for i in range(1, n_dp):
            shid_copy(i, dp_from(i), me_dp).wait_recv()
        shared_out_copy.wait()
        acc[...] = jnp.dot(
            shid[...].reshape(rows, shared_width), sout_v[...], preferred_element_type=F32)

    lag = 3

    @pl.loop(0, chunks + lag)
    def _(c):
        @pl.when(c < chunks)
        def _():
            first(c)

        @pl.when(c == 0)
        def _():
            shared_middle()

        @pl.when((c >= 1) & (c <= chunks))
        def _():
            middle(c - 1)

        @pl.when(c == lag - 1)
        def _():
            shared_last()

        @pl.when(c >= lag)
        def _():
            last(c - lag)

    def pair_copy(i, target):
        return pltpu.make_async_remote_copy(
            src_ref=osend.at[1 - core, target], dst_ref=opair.at[target],
            send_sem=pair_s.at[i], recv_sem=pair_r.at[i],
            device_id=(me_dp, sibling), device_id_type=MESH)

    def out_copy(i, source, target):
        return pltpu.make_async_remote_copy(
            src_ref=osum.at[target], dst_ref=orecv.at[source],
            send_sem=out_s.at[i], recv_sem=out_r.at[i],
            device_id=(me_dp, 2 * target + core), device_id_type=MESH)

    for q in range(groups):
        osend[q % 2, q // 2] = acc[q * rows_dev:(q + 1) * rows_dev, :].astype(BF16)

    def order(i):
        return chip_at(lax.rem(i, chips))

    @pl.loop(1, chips + 1)
    def _(i):
        pair_copy(i - 1, order(i)).start()

    def pair_sum(i):
        target = order(i)
        pair_copy(i - 1, target).wait_recv()
        return osend[core, target].astype(F32) + opair[target].astype(F32)

    @pl.loop(1, chips)
    def _(i):
        osum[chip_at(i)] = pair_sum(i).astype(BF16)
        out_copy(i, chip, chip_at(i)).start()

    total = pair_sum(chips)

    @pl.loop(1, chips)
    def _(i):
        token_copy(i, me, 2 * chip_at(i) + core).wait_send()

    @pl.loop(0, chips)
    def _(i):
        pass_copy(i, 2 * chip_from(i) + core).wait_send()
        pair_copy(i, order(i + 1)).wait_send()

    @pl.loop(1, n_dp)
    def _(i):
        spart_copy(i, me_dp, dp_at(i)).wait_send()
        shid_copy(i, me_dp, dp_at(i)).wait_send()

        @pl.loop(0, chunks)
        def _(c):
            part_copy(c, i, me_dp, dp_at(i)).wait_send()
            hid_copy(c, i, me_dp, dp_at(i)).wait_send()

    for i in range(1, chips):
        out_copy(i, chip_from(i), chip).wait_recv()
        total = total + orecv[chip_from(i)].astype(F32)
    out[...] = total.astype(BF16)

    @pl.loop(1, chips)
    def _(i):
        out_copy(i, chip, chip_at(i)).wait_send()


def per_device(
    tokens, dest_device, local_slot, route_weights, copy_pick, w_in, w_out, shared_in, shared_out
):
    n_dp, groups = lax.axis_size("dp"), lax.axis_size("expert")
    rows_dev, depth = tokens.shape
    experts, _, _, units = w_in.shape
    copies = copy_pick.shape[1]
    shared_units = shared_in.shape[2]
    rows = rows_dev * groups
    mine = rows // n_dp
    chunk = 2 * LANE
    chunks = experts * units // chunk
    table = -(-groups * (experts + copies) // LANE) * LANE
    shared_blocks = max(1, shared_units // (LANE * groups))
    shared_width = shared_blocks * LANE
    shared_active = shared_units // shared_width
    vmem = pl.BlockSpec(memory_space=pltpu.VMEM)
    hbm = pl.BlockSpec(memory_space=pl.ANY)
    dma = pltpu.SemaphoreType.DMA
    dims = (n_dp, groups, experts, copies, chunk, shared_active)
    return pl.pallas_call(
        functools.partial(layer_kernel, dims),
        out_shape=jax.ShapeDtypeStruct((rows_dev, depth), BF16),
        in_specs=[vmem] * 4 + [pl.BlockSpec(memory_space=pltpu.SMEM)] + [hbm] * 4,
        out_specs=vmem,
        scratch_shapes=[
            pltpu.VMEM((groups, rows_dev, depth + 2 * table), BF16),
            pltpu.VMEM((rows, depth + 2 * table), F32),
            pltpu.VMEM((2 * rows, 2 * depth), BF16),
            pltpu.VMEM((experts, rows, LANE), F32),
            pltpu.VMEM((experts, depth, 2, units), BF16),
            pltpu.VMEM((shared_blocks, depth, 2, LANE), BF16),
            pltpu.VMEM((chunks, chunk, depth), BF16),
            pltpu.VMEM((shared_width, depth), BF16),
            pltpu.VMEM((chunks, n_dp, 2, mine, chunk), BF16),
            pltpu.VMEM((chunks, n_dp, 2, mine, chunk), BF16),
            pltpu.VMEM((n_dp, 2, mine, shared_width), BF16),
            pltpu.VMEM((n_dp, 2, mine, shared_width), BF16),
            pltpu.VMEM((chunks, n_dp, mine, chunk), BF16),
            pltpu.VMEM((n_dp, mine, shared_width), BF16),
            pltpu.VMEM((rows, depth), F32),
            pltpu.VMEM((2, groups // 2, rows_dev, depth), BF16),
            pltpu.VMEM((groups // 2, rows_dev, depth), BF16),
            pltpu.VMEM((groups // 2, rows_dev, depth), BF16),
            pltpu.VMEM((groups // 2, rows_dev, depth), BF16),
            dma((experts,)),
            dma((shared_blocks,)),
            dma((chunks,)),
            dma,
            dma((groups // 2,)),
            dma((groups // 2,)),
            dma((groups // 2,)),
            dma((groups // 2,)),
            dma((chunks, n_dp)),
            dma((chunks, n_dp)),
            dma((chunks, n_dp)),
            dma((chunks, n_dp)),
            dma((n_dp,)),
            dma((n_dp,)),
            dma((n_dp,)),
            dma((n_dp,)),
            dma((groups // 2,)),
            dma((groups // 2,)),
            dma((groups // 2,)),
            dma((groups // 2,)),
        ],
        compiler_params=pltpu.CompilerParams(
            collective_id=0, has_side_effects=True, vmem_limit_bytes=56 * 1024 * 1024
        ),
    )(tokens, dest_device, local_slot, route_weights, copy_pick, w_in, w_out, shared_in, shared_out)


def solution(mesh):
    in_specs = (
        P("expert", "dp"),
        P("expert", None),
        P("expert", None),
        P("expert", None),
        P("expert", None),
        P("expert", "dp", None, None),
        P("expert", None, "dp"),
        P("dp", None, None),
        P(None, "dp"),
    )
    out_specs = P("expert", "dp")
    return jax.shard_map(
        per_device, mesh=mesh, in_specs=in_specs, out_specs=out_specs, check_vma=False
    )
```

```python
import functools
import jax
import jax.numpy as jnp
from jax import lax
from jax.experimental import pallas as pl
from jax.experimental.pallas import tpu as pltpu
from jax.sharding import PartitionSpec as P

LANE = 128
MESH = pl.DeviceIdType.MESH
F32 = jnp.float32
BF16 = jnp.bfloat16


def layer_kernel(
    dims, tokens, dest, slot, weights, pick, w_in, w_out, shared_in, shared_out, out,
    gathered, row_block, wide, scale, win_v, sin_v, wout_v, sout_v,
    part, part_in, spart, spart_in, hid, shid, acc, osend, opair, osum, orecv,
    win_sem, sin_sem, wout_sem, sout_sem, tok_s, tok_r, pass_s, pass_r, part_s, part_r, hid_s, hid_r,
    spart_s, spart_r, shid_s, shid_r, pair_s, pair_r, out_s, out_r,
):
    n_dp, groups, experts, copies, chunk, shared_active = dims
    rows_dev, depth = tokens.shape
    rows = rows_dev * groups
    mine = rows // n_dp
    per_expert = w_in.shape[3] // chunk
    chunks = experts * per_expert
    units = w_in.shape[3]
    table = (gathered.shape[2] - depth) // 2
    slots = experts + copies
    me_dp, me = lax.axis_index("dp"), lax.axis_index("expert")

    def dp_at(step):
        return lax.rem(me_dp + step, n_dp)

    def dp_from(step):
        return lax.rem(me_dp + n_dp - step, n_dp)

    chips = groups // 2
    core = lax.rem(me, 2)
    chip = me // 2
    sibling = 2 * chip + 1 - core

    def chip_at(step):
        return lax.rem(chip + step, chips)

    def chip_from(step):
        return lax.rem(chip + chips - step, chips)

    shared_width = sin_v.shape[0] * LANE
    shared_blocks = shared_in.shape[2] // shared_width
    shared_at = pl.multiple_of(lax.rem(me, shared_blocks) * shared_width, LANE)

    def shared_in_copy(half):
        return pltpu.make_async_copy(
            shared_in.at[:, :, pl.ds(pl.multiple_of(shared_at + half * LANE, LANE), LANE)],
            sin_v.at[half], sin_sem.at[half])

    def win_copy(e):
        return pltpu.make_async_copy(w_in.at[e], win_v.at[e], win_sem.at[e])

    def wout_copy(c):
        e, f = c // per_expert, lax.rem(c, per_expert)
        start = pl.multiple_of(f * chunk, chunk)
        return pltpu.make_async_copy(
            w_out.at[e, pl.ds(start, chunk), :], wout_v.at[c], wout_sem.at[c])

    shared_out_copy = pltpu.make_async_copy(
        shared_out.at[pl.ds(shared_at, shared_width), :], sout_v, sout_sem)

    for half in range(sin_v.shape[0]):
        shared_in_copy(half).start()

    win_copy(0).start()

    barrier = pltpu.get_barrier_semaphore()

    pl.semaphore_signal(barrier, inc=1, device_id=(me_dp, sibling), device_id_type=MESH)

    @pl.loop(1, chips)
    def _(i):
        pl.semaphore_signal(
            barrier, inc=1, device_id=(me_dp, 2 * chip_at(i) + core), device_id_type=MESH)

    @pl.loop(1, n_dp)
    def _(i):
        pl.semaphore_signal(barrier, inc=1, device_id=(dp_at(i), me), device_id_type=MESH)

    raw = weights[...]
    norm = raw / jnp.sum(raw, axis=1, keepdims=True)
    key = dest[...] * slots + slot[...]
    lanes = lax.broadcasted_iota(jnp.int32, (rows_dev, table), 1)
    spread = jnp.zeros((rows_dev, table), F32)
    for k in range(key.shape[1]):
        spread = spread + jnp.where(lanes == key[:, k:k + 1], norm[:, k:k + 1], 0.0)
    high = spread.astype(BF16)
    low = (spread - high.astype(F32)).astype(BF16)
    gathered[me] = jnp.concatenate([tokens[...], high, low], axis=1)

    pl.semaphore_wait(barrier, chips + n_dp - 1)

    def token_copy(i, block, target):
        return pltpu.make_async_remote_copy(
            src_ref=gathered.at[block], dst_ref=gathered.at[block],
            send_sem=tok_s.at[i], recv_sem=tok_r.at[i],
            device_id=(me_dp, target), device_id_type=MESH)

    def pass_copy(i, block):
        return pltpu.make_async_remote_copy(
            src_ref=gathered.at[block], dst_ref=gathered.at[block],
            send_sem=pass_s.at[i], recv_sem=pass_r.at[i],
            device_id=(me_dp, sibling), device_id_type=MESH)

    @pl.loop(1, chips)
    def _(i):
        token_copy(i, me, 2 * chip_at(i) + core).start()

    pass_copy(0, me).start()

    @pl.loop(1, experts)
    def _(e):
        win_copy(e).start()

    shared_out_copy.start()

    @pl.loop(0, chunks)
    def _(c):
        wout_copy(c).start()

    at_row = lax.broadcasted_iota(jnp.int32, (LANE, 4 * LANE), 0)
    at_col = lax.broadcasted_iota(jnp.int32, (LANE, 4 * LANE), 1)
    goal = jnp.where(at_col < 2 * LANE, 2 * at_row, 2 * at_row + 1 + 2 * LANE)
    spreader = jnp.where(at_col == goal, 1.0, 0.0).astype(BF16)

    @pl.loop(1, chips)
    def _(i):
        block = 2 * chip_from(i) + core
        token_copy(i, block, me).wait_recv()
        pass_copy(i, block).start()

    @pl.loop(0, chips)
    def _(i):
        pass_copy(i, 2 * chip_from(i) + 1 - core).wait_recv()

    for q in range(groups):
        row_block[q * rows_dev:(q + 1) * rows_dev, :] = gathered[q].astype(F32)

    at_once = max(n for n in (1, 2, 4) if depth // LANE % n == 0)
    for first_block in range(0, depth // LANE, at_once):
        stack = jnp.concatenate(
            [row_block[:, b * LANE:(b + 1) * LANE].astype(BF16)
             for b in range(first_block, first_block + at_once)], axis=0)
        both = jnp.dot(stack, spreader, preferred_element_type=F32).astype(BF16)
        for n in range(at_once):
            b = first_block + n
            part_rows = both[n * rows:(n + 1) * rows]
            wide[0:rows, 2 * b * LANE:2 * (b + 1) * LANE] = part_rows[:, :2 * LANE]
            wide[rows:, 2 * b * LANE:2 * (b + 1) * LANE] = part_rows[:, 2 * LANE:]

    total = row_block[:, depth:depth + table] + row_block[:, depth + table:]
    lanes = lax.broadcasted_iota(jnp.int32, (rows, table), 1)
    for e in range(experts):
        keep = jnp.where(lanes == me * slots + e, 1.0, 0.0)
        for r in range(copies):
            taken = jnp.where(pick[0, r] == e, 1.0, 0.0)
            at = lax.rem(me + r + 1, groups) * slots + experts + r
            keep = keep + jnp.where(lanes == at, taken, 0.0)
        value = jnp.sum(total * keep, axis=1, keepdims=True)
        scale[e] = jnp.broadcast_to(value, (rows, LANE))

    def part_copy(c, i, source, target):
        return pltpu.make_async_remote_copy(
            src_ref=part.at[c, target], dst_ref=part_in.at[c, source],
            send_sem=part_s.at[c, i], recv_sem=part_r.at[c, i],
            device_id=(target, me), device_id_type=MESH)

    def hid_copy(c, i, source, target):
        return pltpu.make_async_remote_copy(
            src_ref=hid.at[c, source], dst_ref=hid.at[c, source],
            send_sem=hid_s.at[c, i], recv_sem=hid_r.at[c, i],
            device_id=(target, me), device_id_type=MESH)

    def spart_copy(i, source, target):
        return pltpu.make_async_remote_copy(
            src_ref=spart.at[target], dst_ref=spart_in.at[source],
            send_sem=spart_s.at[i], recv_sem=spart_r.at[i],
            device_id=(target, me), device_id_type=MESH)

    def shid_copy(i, source, target):
        return pltpu.make_async_remote_copy(
            src_ref=shid.at[source], dst_ref=shid.at[source],
            send_sem=shid_s.at[i], recv_sem=shid_r.at[i],
            device_id=(target, me), device_id_type=MESH)

    def flat(ref):
        return ref.reshape(2 * depth, LANE)[...]

    def project(blocks):
        matrix = blocks[0] if len(blocks) == 1 else jnp.concatenate(blocks, axis=1)
        value = jnp.dot(wide[...], matrix, preferred_element_type=F32)
        return value.astype(BF16).reshape(2, n_dp, mine, matrix.shape[1])

    def activated(total):
        gate, up = total[0], total[1]
        return gate / (1.0 + jnp.exp(-gate)) * up

    for half in range(sin_v.shape[0]):
        shared_in_copy(half).wait()
    value = project([flat(sin_v.at[half]) for half in range(sin_v.shape[0])])
    for p in range(n_dp):
        spart[p] = value[:, p]

    @pl.loop(1, n_dp)
    def _(i):
        spart_copy(i, me_dp, dp_at(i)).start()

    def first(c):
        e, f = c // per_expert, lax.rem(c, per_expert)
        start = pl.multiple_of(f * chunk, chunk)
        value = project([win_v.at[e].reshape(2 * depth, units)[:, pl.ds(start, chunk)]])
        for p in range(n_dp):
            part[c, p] = value[:, p]

    def send_first(c):
        @pl.loop(1, n_dp)
        def _(i):
            part_copy(c, i, me_dp, dp_at(i)).start()

    def wait_first(c):
        e, f = c // per_expert, lax.rem(c, per_expert)

        @pl.when(f == 0)
        def _():
            win_copy(e).wait()

    def wait_middle(c):
        @pl.loop(1, n_dp)
        def _(i):
            part_copy(c, i, dp_from(i), me_dp).wait_recv()

    def middle(c):
        total = part[c, me_dp].astype(F32)
        for i in range(1, n_dp):
            total = total + part_in[c, dp_from(i)].astype(F32)
        factor = scale[c // per_expert, pl.ds(pl.multiple_of(me_dp * mine, mine), mine), :]
        hid[c, me_dp] = (activated(total) * factor[:, :1]).astype(BF16)

    def send_middle(c):
        @pl.loop(1, n_dp)
        def _(i):
            hid_copy(c, i, me_dp, dp_at(i)).start()

    def wait_last(c):
        @pl.loop(1, n_dp)
        def _(i):
            hid_copy(c, i, dp_from(i), me_dp).wait_recv()

        wout_copy(c).wait()

    def last(c):
        return jnp.dot(hid[c].reshape(rows, chunk), wout_v[c], preferred_element_type=F32)

    def shared_middle():
        total = spart[me_dp].astype(F32)
        for i in range(1, n_dp):
            spart_copy(i, dp_from(i), me_dp).wait_recv()
            total = total + spart_in[dp_from(i)].astype(F32)
        active = jnp.where(me < shared_active, 1.0, 0.0)
        shid[me_dp] = (activated(total) * active).astype(BF16)

        @pl.loop(1, n_dp)
        def _(i):
            shid_copy(i, me_dp, dp_at(i)).start()

    def shared_last():
        for i in range(1, n_dp):
            shid_copy(i, dp_from(i), me_dp).wait_recv()
        shared_out_copy.wait()
        acc[...] = jnp.dot(
            shid[...].reshape(rows, shared_width), sout_v[...], preferred_element_type=F32)

    lag = 3
    for at in range(lag):
        c = jnp.int32(at)
        wait_first(c)
        if at == 1:
            shared_middle()
        if at >= 1:
            wait_middle(c - 1)
        first(c)
        if at >= 1:
            middle(c - 1)
        send_first(c)
        if at >= 1:
            send_middle(c - 1)
    shared_last()

    @pl.loop(lag, chunks)
    def _(c):
        wait_first(c)
        wait_middle(c - 1)
        wait_last(c - lag)
        first(c)
        middle(c - 1)
        acc[...] += last(c - lag)
        send_first(c)
        send_middle(c - 1)

    end = jnp.int32(chunks)
    wait_last(end - 3)
    acc[...] += last(end - 3)
    wait_middle(end - 1)
    middle(end - 1)
    send_middle(end - 1)
    wait_last(end - 2)
    acc[...] += last(end - 2)
    wait_last(end - 1)
    acc[...] += last(end - 1)

    def pair_copy(i, target):
        return pltpu.make_async_remote_copy(
            src_ref=osend.at[1 - core, target], dst_ref=opair.at[target],
            send_sem=pair_s.at[i], recv_sem=pair_r.at[i],
            device_id=(me_dp, sibling), device_id_type=MESH)

    def out_copy(i, source, target):
        return pltpu.make_async_remote_copy(
            src_ref=osum.at[target], dst_ref=orecv.at[source],
            send_sem=out_s.at[i], recv_sem=out_r.at[i],
            device_id=(me_dp, 2 * target + core), device_id_type=MESH)

    for q in range(groups):
        osend[q % 2, q // 2] = acc[q * rows_dev:(q + 1) * rows_dev, :].astype(BF16)

    def order(i):
        return chip_at(lax.rem(i, chips))

    @pl.loop(1, chips + 1)
    def _(i):
        pair_copy(i - 1, order(i)).start()

    def pair_sum(i):
        target = order(i)
        pair_copy(i - 1, target).wait_recv()
        return osend[core, target].astype(F32) + opair[target].astype(F32)

    @pl.loop(1, chips)
    def _(i):
        osum[chip_at(i)] = pair_sum(i).astype(BF16)
        out_copy(i, chip, chip_at(i)).start()

    total = pair_sum(chips)

    @pl.loop(1, chips)
    def _(i):
        token_copy(i, me, 2 * chip_at(i) + core).wait_send()

    @pl.loop(0, chips)
    def _(i):
        pass_copy(i, 2 * chip_from(i) + core).wait_send()
        pair_copy(i, order(i + 1)).wait_send()

    @pl.loop(1, n_dp)
    def _(i):
        spart_copy(i, me_dp, dp_at(i)).wait_send()
        shid_copy(i, me_dp, dp_at(i)).wait_send()

        @pl.loop(0, chunks)
        def _(c):
            part_copy(c, i, me_dp, dp_at(i)).wait_send()
            hid_copy(c, i, me_dp, dp_at(i)).wait_send()

    for i in range(1, chips):
        out_copy(i, chip_from(i), chip).wait_recv()
        total = total + orecv[chip_from(i)].astype(F32)
    out[...] = total

    @pl.loop(1, chips)
    def _(i):
        out_copy(i, chip, chip_at(i)).wait_send()


def per_device(
    tokens, dest_device, local_slot, route_weights, copy_pick, w_in, w_out, shared_in, shared_out
):
    n_dp, groups = lax.axis_size("dp"), lax.axis_size("expert")
    rows_dev, depth = tokens.shape
    experts, _, _, units = w_in.shape
    copies = copy_pick.shape[1]
    shared_units = shared_in.shape[2]
    rows = rows_dev * groups
    mine = rows // n_dp
    chunk = 2 * LANE
    chunks = experts * units // chunk
    table = -(-groups * (experts + copies) // LANE) * LANE
    shared_blocks = max(1, shared_units // (LANE * groups))
    shared_width = shared_blocks * LANE
    shared_active = shared_units // shared_width
    vmem = pl.BlockSpec(memory_space=pltpu.VMEM)
    hbm = pl.BlockSpec(memory_space=pl.ANY)
    dma = pltpu.SemaphoreType.DMA
    dims = (n_dp, groups, experts, copies, chunk, shared_active)
    return pl.pallas_call(
        functools.partial(layer_kernel, dims),
        out_shape=jax.ShapeDtypeStruct((rows_dev, depth), F32),
        in_specs=[vmem] * 4 + [pl.BlockSpec(memory_space=pltpu.SMEM)] + [hbm] * 4,
        out_specs=vmem,
        scratch_shapes=[
            pltpu.VMEM((groups, rows_dev, depth + 2 * table), BF16),
            pltpu.VMEM((rows, depth + 2 * table), F32),
            pltpu.VMEM((2 * rows, 2 * depth), BF16),
            pltpu.VMEM((experts, rows, LANE), F32),
            pltpu.VMEM((experts, depth, 2, units), BF16),
            pltpu.VMEM((shared_blocks, depth, 2, LANE), BF16),
            pltpu.VMEM((chunks, chunk, depth), BF16),
            pltpu.VMEM((shared_width, depth), BF16),
            pltpu.VMEM((chunks, n_dp, 2, mine, chunk), BF16),
            pltpu.VMEM((chunks, n_dp, 2, mine, chunk), BF16),
            pltpu.VMEM((n_dp, 2, mine, shared_width), BF16),
            pltpu.VMEM((n_dp, 2, mine, shared_width), BF16),
            pltpu.VMEM((chunks, n_dp, mine, chunk), BF16),
            pltpu.VMEM((n_dp, mine, shared_width), BF16),
            pltpu.VMEM((rows, depth), F32),
            pltpu.VMEM((2, groups // 2, rows_dev, depth), BF16),
            pltpu.VMEM((groups // 2, rows_dev, depth), BF16),
            pltpu.VMEM((groups // 2, rows_dev, depth), BF16),
            pltpu.VMEM((groups // 2, rows_dev, depth), BF16),
            dma((experts,)),
            dma((shared_blocks,)),
            dma((chunks,)),
            dma,
            dma((groups // 2,)),
            dma((groups // 2,)),
            dma((groups // 2,)),
            dma((groups // 2,)),
            dma((chunks, n_dp)),
            dma((chunks, n_dp)),
            dma((chunks, n_dp)),
            dma((chunks, n_dp)),
            dma((n_dp,)),
            dma((n_dp,)),
            dma((n_dp,)),
            dma((n_dp,)),
            dma((groups // 2,)),
            dma((groups // 2,)),
            dma((groups // 2,)),
            dma((groups // 2,)),
        ],
        compiler_params=pltpu.CompilerParams(
            collective_id=0, has_side_effects=True, vmem_limit_bytes=56 * 1024 * 1024
        ),
    )(
        tokens, dest_device, local_slot, route_weights, copy_pick, w_in, w_out, shared_in, shared_out
    ).astype(BF16)


def solution(mesh):
    in_specs = (
        P("expert", "dp"),
        P("expert", None),
        P("expert", None),
        P("expert", None),
        P("expert", None),
        P("expert", "dp", None, None),
        P("expert", None, "dp"),
        P("dp", None, None),
        P(None, "dp"),
    )
    out_specs = P("expert", "dp")
    return jax.shard_map(
        per_device, mesh=mesh, in_specs=in_specs, out_specs=out_specs, check_vma=False
    )
```

```python
import functools
import jax
import jax.numpy as jnp
from jax import lax
from jax.experimental import pallas as pl
from jax.experimental.pallas import tpu as pltpu
from jax.sharding import PartitionSpec as P

LANE = 128
MESH = pl.DeviceIdType.MESH
F32 = jnp.float32
BF16 = jnp.bfloat16


def layer_kernel(
    dims, tokens, dest, slot, weights, pick, w_in, w_out, shared_in, shared_out, out,
    gathered, row_block, wide, scale, win_v, wout_v,
    part, part_in, hid, acc, osend, opair, osum, orecv,
    win_sem, wout_sem, tok_s, tok_r, pass_s, pass_r, part_s, part_r, hid_s, hid_r,
    pair_s, pair_r, out_s, out_r,
):
    n_dp, groups, experts, copies, chunk, shared_active = dims
    rows_dev, depth = tokens.shape
    rows = rows_dev * groups
    mine = rows // n_dp
    per_expert = w_in.shape[3] // chunk
    chunks = experts * per_expert
    units = w_in.shape[3]
    table = (gathered.shape[2] - depth) // 2
    slots = experts + copies
    me_dp, me = lax.axis_index("dp"), lax.axis_index("expert")

    def dp_at(step):
        return lax.rem(me_dp + step, n_dp)

    def dp_from(step):
        return lax.rem(me_dp + n_dp - step, n_dp)

    chips = groups // 2
    core = lax.rem(me, 2)
    chip = me // 2
    sibling = 2 * chip + 1 - core

    def chip_at(step):
        return lax.rem(chip + step, chips)

    def chip_from(step):
        return lax.rem(chip + chips - step, chips)

    shared_blocks = shared_in.shape[2] // LANE
    shared_at = lax.rem(me, shared_blocks)
    own_half = lax.rem(shared_at, 2)
    pair_at = pl.multiple_of((shared_at // 2) * chunk, chunk)
    shared_out_at = pl.multiple_of(shared_at * LANE, LANE)
    own_rows = pl.ds(pl.multiple_of(own_half * LANE, LANE), LANE)
    other_rows = pl.ds(pl.multiple_of((1 - own_half) * LANE, LANE), LANE)

    shared_in_copy = pltpu.make_async_copy(
        shared_in.at[:, :, pl.ds(pair_at, chunk)],
        win_v.at[experts, :, :, pl.ds(0, chunk)], win_sem.at[experts])

    def win_copy(e):
        return pltpu.make_async_copy(w_in.at[e], win_v.at[e], win_sem.at[e])

    def wout_copy(c):
        e, f = c // per_expert, lax.rem(c, per_expert)
        start = pl.multiple_of(f * chunk, chunk)
        return pltpu.make_async_copy(
            w_out.at[e, pl.ds(start, chunk), :], wout_v.at[c], wout_sem.at[c])

    shared_out_copy = pltpu.make_async_copy(
        shared_out.at[pl.ds(shared_out_at, LANE), :],
        wout_v.at[chunks, own_rows, :], wout_sem.at[chunks])

    win_copy(0).start()

    barrier = pltpu.get_barrier_semaphore()

    pl.semaphore_signal(barrier, inc=1, device_id=(me_dp, sibling), device_id_type=MESH)

    @pl.loop(1, chips)
    def _(i):
        pl.semaphore_signal(
            barrier, inc=1, device_id=(me_dp, 2 * chip_at(i) + core), device_id_type=MESH)

    @pl.loop(1, n_dp)
    def _(i):
        pl.semaphore_signal(barrier, inc=1, device_id=(dp_at(i), me), device_id_type=MESH)

    acc[...] = jnp.zeros_like(acc)
    wout_v[chunks, other_rows, :] = jnp.zeros((LANE, depth), BF16)
    raw = weights[...]
    norm = raw / jnp.sum(raw, axis=1, keepdims=True)
    key = dest[...] * slots + slot[...]
    lanes = lax.broadcasted_iota(jnp.int32, (rows_dev, table), 1)
    spread = jnp.zeros((rows_dev, table), F32)
    for k in range(key.shape[1]):
        spread = spread + jnp.where(lanes == key[:, k:k + 1], norm[:, k:k + 1], 0.0)
    high = spread.astype(BF16)
    low = (spread - high.astype(F32)).astype(BF16)
    gathered[me] = jnp.concatenate([tokens[...], high, low], axis=1)

    pl.semaphore_wait(barrier, chips + n_dp - 1)

    def token_copy(i, block, target):
        return pltpu.make_async_remote_copy(
            src_ref=gathered.at[block], dst_ref=gathered.at[block],
            send_sem=tok_s.at[i], recv_sem=tok_r.at[i],
            device_id=(me_dp, target), device_id_type=MESH)

    def pass_copy(i, block):
        return pltpu.make_async_remote_copy(
            src_ref=gathered.at[block], dst_ref=gathered.at[block],
            send_sem=pass_s.at[i], recv_sem=pass_r.at[i],
            device_id=(me_dp, sibling), device_id_type=MESH)

    @pl.loop(1, chips)
    def _(i):
        token_copy(i, me, 2 * chip_at(i) + core).start()

    pass_copy(0, me).start()

    @pl.loop(1, experts)
    def _(e):
        win_copy(e).start()

    shared_in_copy.start()

    @pl.loop(0, chunks)
    def _(c):
        wout_copy(c).start()

    shared_out_copy.start()

    at_row = lax.broadcasted_iota(jnp.int32, (LANE, 4 * LANE), 0)
    at_col = lax.broadcasted_iota(jnp.int32, (LANE, 4 * LANE), 1)
    goal = jnp.where(at_col < 2 * LANE, 2 * at_row, 2 * at_row + 1 + 2 * LANE)
    spreader = jnp.where(at_col == goal, 1.0, 0.0).astype(BF16)

    @pl.loop(1, chips)
    def _(i):
        block = 2 * chip_from(i) + core
        token_copy(i, block, me).wait_recv()
        pass_copy(i, block).start()

    @pl.loop(0, chips)
    def _(i):
        pass_copy(i, 2 * chip_from(i) + 1 - core).wait_recv()

    together = 8 // rows_dev

    @pl.loop(0, groups // together)
    def _(j):
        blocks = [gathered[j * together + n].astype(F32) for n in range(together)]
        row_block[pl.ds(pl.multiple_of(8 * j, 8), 8), :] = jnp.concatenate(blocks, axis=0)

    at_once = max(n for n in (1, 2, 4) if depth // LANE % n == 0)

    @pl.loop(0, depth // LANE // at_once)
    def _(j):
        span = at_once * LANE
        block = row_block[:, pl.ds(pl.multiple_of(j * span, span), span)].astype(BF16)
        stack = jnp.concatenate(
            [block[:, n * LANE:(n + 1) * LANE] for n in range(at_once)], axis=0)
        both = jnp.dot(stack, spreader, preferred_element_type=F32).astype(BF16)
        for n in range(at_once):
            at = pl.ds(pl.multiple_of(2 * j * span + 2 * n * LANE, 2 * LANE), 2 * LANE)
            wide[0:rows, at] = both[n * rows:(n + 1) * rows, :2 * LANE]
            wide[rows:, at] = both[n * rows:(n + 1) * rows, 2 * LANE:]

    total = row_block[:, depth:depth + table] + row_block[:, depth + table:]
    lanes = lax.broadcasted_iota(jnp.int32, (rows, table), 1)
    for e in range(experts):
        keep = jnp.where(lanes == me * slots + e, 1.0, 0.0)
        for r in range(copies):
            taken = jnp.where(pick[0, r] == e, 1.0, 0.0)
            at = lax.rem(me + r + 1, groups) * slots + experts + r
            keep = keep + jnp.where(lanes == at, taken, 0.0)
        value = jnp.sum(total * keep, axis=1, keepdims=True)
        scale[e] = jnp.broadcast_to(value, (rows, LANE))
    scale[experts] = jnp.broadcast_to(jnp.where(me < shared_active, 1.0, 0.0), (rows, LANE))

    def part_copy(c, i, source, target):
        return pltpu.make_async_remote_copy(
            src_ref=part.at[c, target], dst_ref=part_in.at[c, source],
            send_sem=part_s.at[c, i], recv_sem=part_r.at[c, i],
            device_id=(target, me), device_id_type=MESH)

    def hid_copy(c, i, source, target):
        return pltpu.make_async_remote_copy(
            src_ref=hid.at[c, source], dst_ref=hid.at[c, source],
            send_sem=hid_s.at[c, i], recv_sem=hid_r.at[c, i],
            device_id=(target, me), device_id_type=MESH)

    def activated(total):
        gate, up = total[0], total[1]
        return gate / (1.0 + jnp.exp(-gate)) * up

    def first(c):
        e, f = c // per_expert, lax.rem(c, per_expert)

        @pl.when((f == 0) & (e < experts))
        def _():
            win_copy(e).wait()

        @pl.when(e == experts)
        def _():
            shared_in_copy.wait()

        start = pl.multiple_of(f * chunk, chunk)
        matrix = win_v.at[e].reshape(2 * depth, units)

        def some(k, total):
            at = pl.ds(pl.multiple_of(k * span, span), span)
            return total + jnp.dot(
                wide[:, at], matrix[at, pl.ds(start, chunk)], preferred_element_type=F32)

        span = 2 * depth // min(2, 2 * depth // (2 * LANE))
        value = lax.fori_loop(0, 2 * depth // span, some, jnp.zeros((2 * rows, chunk), F32))
        value = value.astype(BF16).reshape(2, n_dp, mine, chunk)
        for p in range(n_dp):
            part[c, p] = value[:, p]

        @pl.loop(1, n_dp)
        def _(i):
            part_copy(c, i, me_dp, dp_at(i)).start()

    def middle(c):
        total = part[c, me_dp].astype(F32)
        for i in range(1, n_dp):
            part_copy(c, i, dp_from(i), me_dp).wait_recv()
            total = total + part_in[c, dp_from(i)].astype(F32)
        factor = scale[c // per_expert, pl.ds(pl.multiple_of(me_dp * mine, mine), mine), :]
        hid[c, me_dp] = (activated(total) * factor[:, :1]).astype(BF16)

        @pl.loop(1, n_dp)
        def _(i):
            hid_copy(c, i, me_dp, dp_at(i)).start()

    def last(c):
        for i in range(1, n_dp):
            hid_copy(c, i, dp_from(i), me_dp).wait_recv()

        @pl.when(c < chunks)
        def _():
            wout_copy(c).wait()

        @pl.when(c == chunks)
        def _():
            shared_out_copy.wait()

        hidden = hid[c].reshape(rows, chunk)
        span = depth // min(2, depth // (2 * LANE))

        @pl.loop(0, depth // span)
        def _(n):
            at = pl.ds(pl.multiple_of(n * span, span), span)
            acc[:, at] += jnp.dot(hidden, wout_v[c, :, at], preferred_element_type=F32)

    lag = 3

    @pl.loop(0, chunks + 1 + lag)
    def _(c):
        @pl.when(c <= chunks)
        def _():
            first(c)

        @pl.when((c >= 1) & (c <= chunks + 1))
        def _():
            middle(c - 1)

        @pl.when(c >= lag)
        def _():
            last(c - lag)

    def pair_copy(i, target):
        return pltpu.make_async_remote_copy(
            src_ref=osend.at[1 - core, target], dst_ref=opair.at[target],
            send_sem=pair_s.at[i], recv_sem=pair_r.at[i],
            device_id=(me_dp, sibling), device_id_type=MESH)

    def out_copy(i, source, target):
        return pltpu.make_async_remote_copy(
            src_ref=osum.at[target], dst_ref=orecv.at[source],
            send_sem=out_s.at[i], recv_sem=out_r.at[i],
            device_id=(me_dp, 2 * target + core), device_id_type=MESH)

    @pl.loop(0, groups // together)
    def _(j):
        block = acc[pl.ds(pl.multiple_of(8 * j, 8), 8), :]
        for n in range(together):
            q = j * together + n
            osend[lax.rem(q, 2), q // 2] = block[n * rows_dev:(n + 1) * rows_dev].astype(BF16)

    def order(i):
        return chip_at(lax.rem(i, chips))

    @pl.loop(1, chips + 1)
    def _(i):
        pair_copy(i - 1, order(i)).start()

    def pair_sum(i):
        target = order(i)
        pair_copy(i - 1, target).wait_recv()
        return osend[core, target].astype(F32) + opair[target].astype(F32)

    @pl.loop(1, chips)
    def _(i):
        osum[chip_at(i)] = pair_sum(i).astype(BF16)
        out_copy(i, chip, chip_at(i)).start()

    total = pair_sum(chips)

    @pl.loop(1, chips)
    def _(i):
        token_copy(i, me, 2 * chip_at(i) + core).wait_send()

    @pl.loop(0, chips)
    def _(i):
        pass_copy(i, 2 * chip_from(i) + core).wait_send()
        pair_copy(i, order(i + 1)).wait_send()

    @pl.loop(1, n_dp)
    def _(i):
        @pl.loop(0, chunks + 1)
        def _(c):
            part_copy(c, i, me_dp, dp_at(i)).wait_send()
            hid_copy(c, i, me_dp, dp_at(i)).wait_send()

    def add(i, total):
        out_copy(i, chip_from(i), chip).wait_recv()
        return total + orecv[chip_from(i)].astype(F32)

    out[...] = lax.fori_loop(1, chips, add, total).astype(BF16)

    @pl.loop(1, chips)
    def _(i):
        out_copy(i, chip, chip_at(i)).wait_send()


def per_device(
    tokens, dest_device, local_slot, route_weights, copy_pick, w_in, w_out, shared_in, shared_out
):
    n_dp, groups = lax.axis_size("dp"), lax.axis_size("expert")
    rows_dev, depth = tokens.shape
    experts, _, _, units = w_in.shape
    copies = copy_pick.shape[1]
    shared_units = shared_in.shape[2]
    rows = rows_dev * groups
    mine = rows // n_dp
    chunk = 2 * LANE
    chunks = experts * units // chunk
    table = -(-groups * (experts + copies) // LANE) * LANE
    shared_active = shared_units // LANE
    vmem = pl.BlockSpec(memory_space=pltpu.VMEM)
    hbm = pl.BlockSpec(memory_space=pl.ANY)
    dma = pltpu.SemaphoreType.DMA
    dims = (n_dp, groups, experts, copies, chunk, shared_active)
    return pl.pallas_call(
        functools.partial(layer_kernel, dims),
        out_shape=jax.ShapeDtypeStruct((rows_dev, depth), BF16),
        in_specs=[vmem] * 4 + [pl.BlockSpec(memory_space=pltpu.SMEM)] + [hbm] * 4,
        out_specs=vmem,
        scratch_shapes=[
            pltpu.VMEM((groups, rows_dev, depth + 2 * table), BF16),
            pltpu.VMEM((rows, depth + 2 * table), F32),
            pltpu.VMEM((2 * rows, 2 * depth), BF16),
            pltpu.VMEM((experts + 1, rows, LANE), F32),
            pltpu.VMEM((experts + 1, depth, 2, units), BF16),
            pltpu.VMEM((chunks + 1, chunk, depth), BF16),
            pltpu.VMEM((chunks + 1, n_dp, 2, mine, chunk), BF16),
            pltpu.VMEM((chunks + 1, n_dp, 2, mine, chunk), BF16),
            pltpu.VMEM((chunks + 1, n_dp, mine, chunk), BF16),
            pltpu.VMEM((rows, depth), F32),
            pltpu.VMEM((2, groups // 2, rows_dev, depth), BF16),
            pltpu.VMEM((groups // 2, rows_dev, depth), BF16),
            pltpu.VMEM((groups // 2, rows_dev, depth), BF16),
            pltpu.VMEM((groups // 2, rows_dev, depth), BF16),
            dma((experts + 1,)),
            dma((chunks + 1,)),
        ] + [dma((groups // 2,))] * 4 + [dma((chunks + 1, n_dp))] * 4
        + [dma((groups // 2,))] * 4,
        compiler_params=pltpu.CompilerParams(
            collective_id=0, has_side_effects=True, vmem_limit_bytes=56 * 1024 * 1024
        ),
    )(tokens, dest_device, local_slot, route_weights, copy_pick, w_in, w_out, shared_in, shared_out)


def solution(mesh):
    in_specs = (
        P("expert", "dp"),
        P("expert", None),
        P("expert", None),
        P("expert", None),
        P("expert", None),
        P("expert", "dp", None, None),
        P("expert", None, "dp"),
        P("dp", None, None),
        P(None, "dp"),
    )
    out_specs = P("expert", "dp")
    return jax.shard_map(
        per_device, mesh=mesh, in_specs=in_specs, out_specs=out_specs, check_vma=False
    )
```

```python
import functools
import jax
import jax.numpy as jnp
from jax import lax
from jax.experimental import pallas as pl
from jax.experimental.pallas import tpu as pltpu
from jax.sharding import PartitionSpec as P

LANE = 128
MESH = pl.DeviceIdType.MESH
F32 = jnp.float32
BF16 = jnp.bfloat16


def layer_kernel(
    dims, tokens, dest, slot, weights, pick, w_in, w_out, shared_in, shared_out, out,
    gathered, row_block, wide, scale, win_v, sin_v, wout_v, sout_v,
    part, part_in, spart, spart_in, hid, shid, acc, osend, opair, osum, orecv,
    win_sem, sin_sem, wout_sem, sout_sem, tok_s, tok_r, pass_s, pass_r, part_s, part_r, hid_s, hid_r,
    spart_s, spart_r, shid_s, shid_r, pair_s, pair_r, out_s, out_r,
):
    n_dp, groups, experts, copies, chunk, shared_active = dims
    rows_dev, depth = tokens.shape
    rows = rows_dev * groups
    mine = rows // n_dp
    per_expert = w_in.shape[3] // chunk
    chunks = experts * per_expert
    units = w_in.shape[3]
    table = (gathered.shape[2] - depth) // 2
    slots = experts + copies
    me_dp, me = lax.axis_index("dp"), lax.axis_index("expert")

    def dp_at(step):
        return lax.rem(me_dp + step, n_dp)

    def dp_from(step):
        return lax.rem(me_dp + n_dp - step, n_dp)

    chips = groups // 2
    core = lax.rem(me, 2)
    chip = me // 2
    sibling = 2 * chip + 1 - core

    def chip_at(step):
        return lax.rem(chip + step, chips)

    def chip_from(step):
        return lax.rem(chip + chips - step, chips)

    shared_width = sin_v.shape[0] * LANE
    shared_blocks = shared_in.shape[2] // shared_width
    shared_at = pl.multiple_of(lax.rem(me, shared_blocks) * shared_width, LANE)

    def shared_in_copy(half):
        return pltpu.make_async_copy(
            shared_in.at[:, :, pl.ds(pl.multiple_of(shared_at + half * LANE, LANE), LANE)],
            sin_v.at[half], sin_sem.at[half])

    def win_copy(e):
        return pltpu.make_async_copy(
            w_in.at[e], win_v.at[e, :, :, pl.ds(0, units)], win_sem.at[e])

    def wout_copy(c):
        e, f = c // per_expert, lax.rem(c, per_expert)
        start = pl.multiple_of(f * chunk, chunk)
        return pltpu.make_async_copy(
            w_out.at[e, pl.ds(start, chunk), :], wout_v.at[c], wout_sem.at[c])

    shared_out_copy = pltpu.make_async_copy(
        shared_out.at[pl.ds(shared_at, shared_width), :], sout_v, sout_sem)

    for half in range(sin_v.shape[0]):
        shared_in_copy(half).start()

    win_copy(0).start()

    barrier = pltpu.get_barrier_semaphore()

    pl.semaphore_signal(barrier, inc=1, device_id=(me_dp, sibling), device_id_type=MESH)

    @pl.loop(1, chips)
    def _(i):
        pl.semaphore_signal(
            barrier, inc=1, device_id=(me_dp, 2 * chip_at(i) + core), device_id_type=MESH)

    @pl.loop(1, n_dp)
    def _(i):
        pl.semaphore_signal(barrier, inc=1, device_id=(dp_at(i), me), device_id_type=MESH)

    raw = weights[...]
    norm = raw / jnp.sum(raw, axis=1, keepdims=True)
    key = dest[...] * slots + slot[...]
    lanes = lax.broadcasted_iota(jnp.int32, (rows_dev, table), 1)
    spread = jnp.zeros((rows_dev, table), F32)
    for k in range(key.shape[1]):
        spread = spread + jnp.where(lanes == key[:, k:k + 1], norm[:, k:k + 1], 0.0)
    high = spread.astype(BF16)
    low = (spread - high.astype(F32)).astype(BF16)
    gathered[me] = jnp.concatenate([tokens[...], high, low], axis=1)

    pl.semaphore_wait(barrier, chips + n_dp - 1)

    def token_copy(i, block, target):
        return pltpu.make_async_remote_copy(
            src_ref=gathered.at[block], dst_ref=gathered.at[block],
            send_sem=tok_s.at[i], recv_sem=tok_r.at[i],
            device_id=(me_dp, target), device_id_type=MESH)

    def pass_copy(i, block):
        return pltpu.make_async_remote_copy(
            src_ref=gathered.at[block], dst_ref=gathered.at[block],
            send_sem=pass_s.at[i], recv_sem=pass_r.at[i],
            device_id=(me_dp, sibling), device_id_type=MESH)

    @pl.loop(1, chips)
    def _(i):
        token_copy(i, me, 2 * chip_at(i) + core).start()

    pass_copy(0, me).start()

    @pl.loop(1, experts)
    def _(e):
        win_copy(e).start()

    shared_out_copy.start()

    @pl.loop(0, chunks)
    def _(c):
        wout_copy(c).start()

    at_row = lax.broadcasted_iota(jnp.int32, (LANE, 4 * LANE), 0)
    at_col = lax.broadcasted_iota(jnp.int32, (LANE, 4 * LANE), 1)
    goal = jnp.where(at_col < 2 * LANE, 2 * at_row, 2 * at_row + 1 + 2 * LANE)
    spreader = jnp.where(at_col == goal, 1.0, 0.0).astype(BF16)

    @pl.loop(1, chips)
    def _(i):
        block = 2 * chip_from(i) + core
        token_copy(i, block, me).wait_recv()
        pass_copy(i, block).start()

    @pl.loop(0, chips)
    def _(i):
        pass_copy(i, 2 * chip_from(i) + 1 - core).wait_recv()

    for q in range(groups):
        row_block[q * rows_dev:(q + 1) * rows_dev, :] = gathered[q].astype(F32)

    for b in range(depth // LANE):
        block = row_block[:, b * LANE:(b + 1) * LANE].astype(BF16)
        both = jnp.dot(block, spreader, preferred_element_type=F32).astype(BF16)
        wide[0:rows, 2 * b * LANE:2 * (b + 1) * LANE] = both[:, :2 * LANE]
        wide[rows:, 2 * b * LANE:2 * (b + 1) * LANE] = both[:, 2 * LANE:]

    total = row_block[:, depth:depth + table] + row_block[:, depth + table:]
    lanes = lax.broadcasted_iota(jnp.int32, (rows, table), 1)
    for e in range(experts):
        keep = jnp.where(lanes == me * slots + e, 1.0, 0.0)
        for r in range(copies):
            taken = jnp.where(pick[0, r] == e, 1.0, 0.0)
            at = lax.rem(me + r + 1, groups) * slots + experts + r
            keep = keep + jnp.where(lanes == at, taken, 0.0)
        value = jnp.sum(total * keep, axis=1, keepdims=True)
        scale[e] = jnp.broadcast_to(value, (rows, LANE))

    def part_copy(c, i, source, target):
        return pltpu.make_async_remote_copy(
            src_ref=part.at[c, target], dst_ref=part_in.at[c, source],
            send_sem=part_s.at[c, i], recv_sem=part_r.at[c, i],
            device_id=(target, me), device_id_type=MESH)

    def hid_copy(c, i, source, target):
        return pltpu.make_async_remote_copy(
            src_ref=hid.at[c, source], dst_ref=hid.at[c, source],
            send_sem=hid_s.at[c, i], recv_sem=hid_r.at[c, i],
            device_id=(target, me), device_id_type=MESH)

    def spart_copy(i, source, target):
        return pltpu.make_async_remote_copy(
            src_ref=spart.at[target], dst_ref=spart_in.at[source],
            send_sem=spart_s.at[i], recv_sem=spart_r.at[i],
            device_id=(target, me), device_id_type=MESH)

    def shid_copy(i, source, target):
        return pltpu.make_async_remote_copy(
            src_ref=shid.at[source], dst_ref=shid.at[source],
            send_sem=shid_s.at[i], recv_sem=shid_r.at[i],
            device_id=(target, me), device_id_type=MESH)

    def flat(ref):
        return ref.reshape(2 * depth, LANE)[...]

    def project(blocks):
        matrix = blocks[0] if len(blocks) == 1 else jnp.concatenate(blocks, axis=1)
        value = jnp.dot(wide[...], matrix, preferred_element_type=F32)
        return value.astype(BF16).reshape(2, n_dp, mine, matrix.shape[1])

    def activated(total):
        gate, up = total[0], total[1]
        return gate / (1.0 + jnp.exp(-gate)) * up

    for half in range(sin_v.shape[0]):
        shared_in_copy(half).wait()
    value = project([flat(sin_v.at[half]) for half in range(sin_v.shape[0])])
    for p in range(n_dp):
        spart[p] = value[:, p]

    @pl.loop(1, n_dp)
    def _(i):
        spart_copy(i, me_dp, dp_at(i)).start()

    def first(c):
        e, f = c // per_expert, lax.rem(c, per_expert)

        @pl.when(f == 0)
        def _():
            win_copy(e).wait()

        start = pl.multiple_of(f * chunk, chunk)
        value = project([win_v.at[e].reshape(2 * depth, units + LANE)[:, pl.ds(start, chunk)]])
        for p in range(n_dp):
            part[c, p] = value[:, p]

        @pl.loop(1, n_dp)
        def _(i):
            part_copy(c, i, me_dp, dp_at(i)).start()

    def middle(c):
        total = part[c, me_dp].astype(F32)
        for i in range(1, n_dp):
            part_copy(c, i, dp_from(i), me_dp).wait_recv()
            total = total + part_in[c, dp_from(i)].astype(F32)
        factor = scale[c // per_expert, pl.ds(pl.multiple_of(me_dp * mine, mine), mine), :]
        hid[c, me_dp] = (activated(total) * factor[:, :1]).astype(BF16)

        @pl.loop(1, n_dp)
        def _(i):
            hid_copy(c, i, me_dp, dp_at(i)).start()

    def shared_middle():
        total = spart[me_dp].astype(F32)
        for i in range(1, n_dp):
            spart_copy(i, dp_from(i), me_dp).wait_recv()
            total = total + spart_in[dp_from(i)].astype(F32)
        active = jnp.where(me < shared_active, 1.0, 0.0)
        shid[me_dp] = (activated(total) * active).astype(BF16)

        @pl.loop(1, n_dp)
        def _(i):
            shid_copy(i, me_dp, dp_at(i)).start()

    def last(c):
        for i in range(1, n_dp):
            hid_copy(c, i, dp_from(i), me_dp).wait_recv()
        wout_copy(c).wait()
        acc[...] += jnp.dot(
            hid[c].reshape(rows, chunk), wout_v[c], preferred_element_type=F32)

    def shared_last():
        for i in range(1, n_dp):
            shid_copy(i, dp_from(i), me_dp).wait_recv()
        shared_out_copy.wait()
        acc[...] = jnp.dot(
            shid[...].reshape(rows, shared_width), sout_v[...], preferred_element_type=F32)

    lag = 3

    @pl.loop(0, chunks + lag)
    def _(c):
        @pl.when(c < chunks)
        def _():
            first(c)

        @pl.when(c == 0)
        def _():
            shared_middle()

        @pl.when((c >= 1) & (c <= chunks))
        def _():
            middle(c - 1)

        @pl.when(c == lag - 1)
        def _():
            shared_last()

        @pl.when(c >= lag)
        def _():
            last(c - lag)

    def pair_copy(i, target):
        return pltpu.make_async_remote_copy(
            src_ref=osend.at[1 - core, target], dst_ref=opair.at[target],
            send_sem=pair_s.at[i], recv_sem=pair_r.at[i],
            device_id=(me_dp, sibling), device_id_type=MESH)

    def out_copy(i, source, target):
        return pltpu.make_async_remote_copy(
            src_ref=osum.at[target], dst_ref=orecv.at[source],
            send_sem=out_s.at[i], recv_sem=out_r.at[i],
            device_id=(me_dp, 2 * target + core), device_id_type=MESH)

    for q in range(groups):
        osend[q % 2, q // 2] = acc[q * rows_dev:(q + 1) * rows_dev, :].astype(BF16)

    def order(i):
        return chip_at(lax.rem(i, chips))

    @pl.loop(1, chips + 1)
    def _(i):
        pair_copy(i - 1, order(i)).start()

    def pair_sum(i):
        target = order(i)
        pair_copy(i - 1, target).wait_recv()
        return osend[core, target].astype(F32) + opair[target].astype(F32)

    @pl.loop(1, chips)
    def _(i):
        osum[chip_at(i)] = pair_sum(i).astype(BF16)
        out_copy(i, chip, chip_at(i)).start()

    total = pair_sum(chips)

    @pl.loop(1, chips)
    def _(i):
        token_copy(i, me, 2 * chip_at(i) + core).wait_send()

    @pl.loop(0, chips)
    def _(i):
        pass_copy(i, 2 * chip_from(i) + core).wait_send()
        pair_copy(i, order(i + 1)).wait_send()

    @pl.loop(1, n_dp)
    def _(i):
        spart_copy(i, me_dp, dp_at(i)).wait_send()
        shid_copy(i, me_dp, dp_at(i)).wait_send()

        @pl.loop(0, chunks)
        def _(c):
            part_copy(c, i, me_dp, dp_at(i)).wait_send()
            hid_copy(c, i, me_dp, dp_at(i)).wait_send()

    for i in range(1, chips):
        out_copy(i, chip_from(i), chip).wait_recv()
        total = total + orecv[chip_from(i)].astype(F32)
    out[...] = total.astype(BF16)

    @pl.loop(1, chips)
    def _(i):
        out_copy(i, chip, chip_at(i)).wait_send()


def per_device(
    tokens, dest_device, local_slot, route_weights, copy_pick, w_in, w_out, shared_in, shared_out
):
    n_dp, groups = lax.axis_size("dp"), lax.axis_size("expert")
    rows_dev, depth = tokens.shape
    experts, _, _, units = w_in.shape
    copies = copy_pick.shape[1]
    shared_units = shared_in.shape[2]
    rows = rows_dev * groups
    mine = rows // n_dp
    chunk = 2 * LANE
    chunks = experts * units // chunk
    table = -(-groups * (experts + copies) // LANE) * LANE
    shared_blocks = max(1, shared_units // (LANE * groups))
    shared_width = shared_blocks * LANE
    shared_active = shared_units // shared_width
    vmem = pl.BlockSpec(memory_space=pltpu.VMEM)
    hbm = pl.BlockSpec(memory_space=pl.ANY)
    dma = pltpu.SemaphoreType.DMA
    dims = (n_dp, groups, experts, copies, chunk, shared_active)
    return pl.pallas_call(
        functools.partial(layer_kernel, dims),
        out_shape=jax.ShapeDtypeStruct((rows_dev, depth), BF16),
        in_specs=[vmem] * 4 + [pl.BlockSpec(memory_space=pltpu.SMEM)] + [hbm] * 4,
        out_specs=vmem,
        scratch_shapes=[
            pltpu.VMEM((groups, rows_dev, depth + 2 * table), BF16),
            pltpu.VMEM((rows, depth + 2 * table), F32),
            pltpu.VMEM((2 * rows, 2 * depth), BF16),
            pltpu.VMEM((experts, rows, LANE), F32),
            pltpu.VMEM((experts, depth, 2, units + LANE), BF16),
            pltpu.VMEM((shared_blocks, depth, 2, LANE), BF16),
            pltpu.VMEM((chunks, chunk, depth), BF16),
            pltpu.VMEM((shared_width, depth), BF16),
            pltpu.VMEM((chunks, n_dp, 2, mine, chunk), BF16),
            pltpu.VMEM((chunks, n_dp, 2, mine, chunk), BF16),
            pltpu.VMEM((n_dp, 2, mine, shared_width), BF16),
            pltpu.VMEM((n_dp, 2, mine, shared_width), BF16),
            pltpu.VMEM((chunks, n_dp, mine, chunk), BF16),
            pltpu.VMEM((n_dp, mine, shared_width), BF16),
            pltpu.VMEM((rows, depth), F32),
            pltpu.VMEM((2, groups // 2, rows_dev, depth), BF16),
            pltpu.VMEM((groups // 2, rows_dev, depth), BF16),
            pltpu.VMEM((groups // 2, rows_dev, depth), BF16),
            pltpu.VMEM((groups // 2, rows_dev, depth), BF16),
            dma((experts,)),
            dma((shared_blocks,)),
            dma((chunks,)),
            dma,
            dma((groups // 2,)),
            dma((groups // 2,)),
            dma((groups // 2,)),
            dma((groups // 2,)),
            dma((chunks, n_dp)),
            dma((chunks, n_dp)),
            dma((chunks, n_dp)),
            dma((chunks, n_dp)),
            dma((n_dp,)),
            dma((n_dp,)),
            dma((n_dp,)),
            dma((n_dp,)),
            dma((groups // 2,)),
            dma((groups // 2,)),
            dma((groups // 2,)),
            dma((groups // 2,)),
        ],
        compiler_params=pltpu.CompilerParams(
            collective_id=0, has_side_effects=True, vmem_limit_bytes=56 * 1024 * 1024
        ),
    )(tokens, dest_device, local_slot, route_weights, copy_pick, w_in, w_out, shared_in, shared_out)


def solution(mesh):
    in_specs = (
        P("expert", "dp"),
        P("expert", None),
        P("expert", None),
        P("expert", None),
        P("expert", None),
        P("expert", "dp", None, None),
        P("expert", None, "dp"),
        P("dp", None, None),
        P(None, "dp"),
    )
    out_specs = P("expert", "dp")
    return jax.shard_map(
        per_device, mesh=mesh, in_specs=in_specs, out_specs=out_specs, check_vma=False
    )
```
